32 devices in a mesh: dom: 8 (over z, x), rep: 4 (over y, core).
Axes of the slice: x: 2, y: 2, z: 4, core: 2. Of those that a mesh axis runs over, the one named last changes fastest.
Arguments:
- features: float32 [128, 4096], P('rep', 'dom'), may hold values from -6 to 6
- tiles: bfloat16 [320, 128, 128], P('dom'), may hold values from -0.25 to 0.25
- tile_row: int32 [320], P('dom'), may hold values from 0 to 3
- tile_col: int32 [320], P('dom'), may hold values from 0 to 31, as said below
- tile_count: int32 [8], P('dom'), may hold values from 16 to 40, as said below
- dest_slot: int32 [4096], P('dom'), may hold values from 0 to 4095, as said below
- w_in: bfloat16 [128, 1024], replicated, may hold values from -0.5 to 0.5
- w_mid: bfloat16 [1024, 1024], replicated, may hold values from -0.1875 to 0.1875
- w_out: bfloat16 [172, 1024], replicated, may hold values from -0.1875 to 0.1875
- cotangent: bfloat16 [172, 4096], P(None, ('dom', 'rep')), may hold values from -0.09375 to 0.09375
Outputs:
- batch_features: float32 [128, 4096], P(None, ('dom', 'rep'))
- grad_w_in: float32 [128, 1024], replicated
- grad_w_mid: float32 [1024, 1024], P('dom')
- grad_w_out: float32 [172, 1024], replicated
The draws below stay inside these ranges and needn't reach their ends.
Inputs may be any that keep to these rules, and one draw needn't show every extreme that they name: `tile_col`: every slot of partition p, live or not, names a block column within 4 blocks of p's own blocks p * 4 to (p+1) * 4 - 1, counted modulo 32; each of the 8 blocks just before and just after p's own is named by one of p's first 8 slots. `tile_count`: counts vary from partition to partition (several partitions may share a count); at least one partition holds exactly 40 live slots. `dest_slot`: A permutation of the batch positions; each graph partition sends exactly 16 node into each block of 128 consecutive batch positions.
All inputs are finite; a program needn't handle non-finite values.
Results may differ from the reference program's by a relative error of at most 0.006.
Values sent between devices are 32-bit elements; how exact they have to be, the bound alone decides.
No kernel may reach another device: no remote copies, remote signals or barrier semaphores. Data moves between devices by JAX's collectives and lax.ppermute only.
A program may use at most 64 MiB of HBM per device.

```python
import jax
import jax.numpy as jnp
from jax import lax

FEAT = 128
TB = 128
BLK_DEV = 4
HALO_B = 4
TILE_CAP = 40
HID = 1024
CLASSES = 172
NODES_DEV = 512
NB = 32
NODES = 4096
TILES = 320
MLP_ROWS = 128
SEG = 16
N_DOM = 8
DEVICES = 32


def draw_tile_row(key, part):
    return jax.random.randint(jax.random.fold_in(key, 11), (TILES,), 0, BLK_DEV, dtype=jnp.int32)


def draw_tile_col(key, part):
    index = jnp.arange(TILES, dtype=jnp.int32)
    owner = index // TILE_CAP
    slot_id = index % TILE_CAP
    spread = jax.random.randint(jax.random.fold_in(key, 12), (TILES,), 0, BLK_DEV + 2 * HALO_B, dtype=jnp.int32)
    offset = jnp.where(slot_id < HALO_B, slot_id, jnp.where(slot_id < 2 * HALO_B, BLK_DEV + slot_id, spread))
    return jnp.mod(owner * BLK_DEV - HALO_B + offset, NB).astype(jnp.int32)


def draw_tile_count(key, part):
    lowest = 2 * HALO_B + 8
    counts = jax.random.randint(jax.random.fold_in(key, 13), (N_DOM,), lowest, lowest + TILE_CAP // 4 + 1, dtype=jnp.int32)
    busiest = jax.random.randint(jax.random.fold_in(key, 14), (), 0, N_DOM, dtype=jnp.int32)
    return jnp.where(jnp.arange(N_DOM, dtype=jnp.int32) == busiest, TILE_CAP, counts).astype(jnp.int32)


def draw_dest_slot(key, part):
    scores = jax.random.randint(jax.random.fold_in(key, 15), (N_DOM, NODES_DEV), 0, 2 ** 14, dtype=jnp.int32)
    scores = scores * NODES_DEV + jnp.arange(NODES_DEV, dtype=jnp.int32)[None, :]
    ranking = jnp.argsort(jnp.argsort(scores, axis=1), axis=1).astype(jnp.int32)
    owner = ranking // SEG
    within = jnp.arange(N_DOM, dtype=jnp.int32)[:, None] * SEG + ranking % SEG
    mixing = jax.random.randint(jax.random.fold_in(key, 16), (DEVICES, MLP_ROWS), 0, 2 ** 14, dtype=jnp.int32)
    mixing = mixing * MLP_ROWS + jnp.arange(MLP_ROWS, dtype=jnp.int32)[None, :]
    shuffle = jnp.argsort(mixing, axis=1).astype(jnp.int32)
    placed_blocks = owner * MLP_ROWS + shuffle[owner, within]
    return placed_blocks.reshape(NODES).astype(jnp.int32)


def shard_levels(key, shape, shards, low, high):
    def one(dim, shards_of):
        steps = jax.random.uniform(jax.random.fold_in(jax.random.fold_in(key, 6), dim), (shards_of,), jnp.float32, low / len(shards), high / len(shards))
        return jnp.repeat(jnp.exp(steps), shape[dim] // shards_of).reshape((-1,) + (1,) * (len(shape) - dim - 1))

    level = one(*shards[0])
    for cut in shards[1:]:
        level = level * one(*cut)
    return level


def normal_values(key, dims, scale, limit, split=(), held_as=jnp.bfloat16):
    level = shard_levels(key, dims, split, -0.22, 0.18) if split else 1.0
    entries = jax.random.normal(key, dims, jnp.float32) * scale * level
    return jnp.minimum(jnp.maximum(entries, -limit), limit).astype(held_as)


def setup_inputs(seed: int = 0) -> dict:
    keys = jax.random.split(jax.random.key(seed), 11)
    return {
        "features": normal_values(keys[0], (FEAT, NODES), 1.0, 6.0, ((0, 4), (1, 8)), jnp.float32),
        "tiles": normal_values(keys[1], (TILES, TB, TB), (4 * TB) ** -0.5, 0.25, ((0, 8),)),
        "tile_row": draw_tile_row(jax.random.fold_in(keys[10], 71), 0),
        "tile_col": draw_tile_col(jax.random.fold_in(keys[10], 71), 0),
        "tile_count": draw_tile_count(jax.random.fold_in(keys[10], 71), 0),
        "dest_slot": draw_dest_slot(jax.random.fold_in(keys[10], 71), 0),
        "w_in": normal_values(keys[6], (FEAT, HID), FEAT ** -0.5, 0.5),
        "w_mid": normal_values(keys[7], (HID, HID), HID ** -0.5, 0.1875),
        "w_out": normal_values(keys[8], (CLASSES, HID), HID ** -0.5, 0.1875),
        "cotangent": normal_values(keys[9], (CLASSES, NODES), (2.0 * NODES ** -0.5), 0.09375, ((1, 32),)),
    }


series_zero = 0.3085083
series_one = -0.4305395
series_two = 0.1864784
LEADING = (((0,), (0,)), ((), ()))
TRAILING = (((1,), (1,)), ((), ()))


def silu_slope(pre):
    sigma = jax.nn.sigmoid(pre)
    return sigma * (1.0 + pre * (1.0 - sigma))


def apply_operator(field, tiles, tile_row, tile_col, tile_count):
    blocks = field.reshape(FEAT, NB, TB)
    tile_groups = tiles.reshape(N_DOM, TILE_CAP, TB, TB)
    row_groups = tile_row.reshape(N_DOM, TILE_CAP)
    col_groups = tile_col.reshape(N_DOM, TILE_CAP)
    slot_ids = jnp.arange(TILE_CAP, dtype=jnp.int32)
    targets = jnp.arange(BLK_DEV, dtype=jnp.int32)

    def one_part(packed):
        partition_tiles, part_rows, part_cols, part_count = packed
        input_values = jnp.take(blocks, part_cols, axis=1)
        block_products = jnp.einsum("lkz,glz->glk", partition_tiles.astype(jnp.float32), input_values, precision=lax.Precision.HIGHEST)
        live_mask = (slot_ids < part_count).astype(jnp.float32)
        assignment_map = (part_rows[None, :] == targets[:, None]).astype(jnp.float32) * live_mask[None, :]
        return jnp.einsum("wy,kya->kwa", assignment_map, block_products, precision=lax.Precision.HIGHEST)

    stacked = lax.map(one_part, (tile_groups, row_groups, col_groups, tile_count))
    return jnp.transpose(stacked, (1, 0, 2, 3)).reshape(FEAT, NODES)


def reference(features, tiles, tile_row, tile_col, tile_count, dest_slot, w_in, w_mid, w_out, cotangent):
    first = apply_operator(features, tiles, tile_row, tile_col, tile_count)
    second = 2.0 * apply_operator(first, tiles, tile_row, tile_col, tile_count) - features
    diffused = series_zero * features + series_one * first + series_two * second
    batch_features = jnp.zeros_like(diffused).at[:, dest_slot].set(diffused)
    inputs_bf = batch_features.astype(jnp.bfloat16)

    def one_block(carry, block_index):
        grad_in, grad_mid, grad_out = carry
        first_row = block_index * MLP_ROWS
        input_block = lax.dynamic_slice_in_dim(inputs_bf, first_row, MLP_ROWS, 1)
        cot_block = lax.dynamic_slice_in_dim(cotangent, first_row, MLP_ROWS, 1)
        pre_one = lax.dot_general(input_block, w_in, LEADING, preferred_element_type=jnp.float32)
        hidden_one = jax.nn.silu(pre_one).astype(jnp.bfloat16)
        pre_two = jnp.dot(hidden_one, w_mid, preferred_element_type=jnp.float32)
        hidden_two = jax.nn.silu(pre_two).astype(jnp.bfloat16)
        out_term = jnp.dot(cot_block, hidden_two, preferred_element_type=jnp.float32)
        back_two = lax.dot_general(cot_block, w_out, LEADING, preferred_element_type=jnp.float32)
        delta_two = (back_two * silu_slope(pre_two)).astype(jnp.bfloat16)
        mid_term = lax.dot_general(hidden_one, delta_two, LEADING, preferred_element_type=jnp.float32)
        back_one = lax.dot_general(delta_two, w_mid, TRAILING, preferred_element_type=jnp.float32)
        delta_one = (back_one * silu_slope(pre_one)).astype(jnp.bfloat16)
        in_term = jnp.dot(input_block, delta_one, preferred_element_type=jnp.float32)
        return (grad_in + in_term, grad_mid + mid_term, grad_out + out_term), None

    start_state = (jnp.zeros((FEAT, HID), jnp.float32), jnp.zeros((HID, HID), jnp.float32), jnp.zeros((CLASSES, HID), jnp.float32))
    totals, unused = lax.scan(one_block, start_state, jnp.arange(DEVICES, dtype=jnp.int32))
    return batch_features, totals[0], totals[1], totals[2]
```

```python
import functools

import jax
import jax.numpy as jnp
from jax import lax
from jax.experimental import pallas as pl
from jax.experimental.pallas import tpu as pltpu
from jax.sharding import PartitionSpec as P

series_zero = 0.3085083
series_one = -0.4305395
series_two = 0.1864784
LEADING = (((0,), (0,)), ((), ()))
TRAILING = (((1,), (1,)), ((), ()))
AXES = ("dom", "rep")
F32 = jnp.float32
BF16 = jnp.bfloat16
VMEM = pl.BlockSpec(memory_space=pltpu.VMEM)
SMEM = pl.BlockSpec(memory_space=pltpu.SMEM)


def pieces(value):
    high = value.astype(BF16)
    rest = value - high.astype(F32)
    middle = rest.astype(BF16)
    low = (rest - middle.astype(F32)).astype(BF16)
    return jnp.concatenate([high, middle, low], axis=0)


def whole(parts):
    rows = parts.shape[0] // 3
    return parts[:rows] + parts[rows : 2 * rows] + parts[2 * rows :]


def prepare_kernel(segment, block, place, slots, cot, packed, rank_row):
    nodes = slots.shape[1]
    half = nodes // 2
    row = slots[...]
    lane = lax.broadcasted_iota(jnp.int32, (nodes, nodes), 1)
    sublane = lax.broadcasted_iota(jnp.int32, (nodes, nodes), 0)
    wide = jnp.broadcast_to(row, (nodes, nodes))
    column = jnp.sum(jnp.where(lane == sublane, wide, 0), axis=1, keepdims=True)

    def position(slot, order):
        target = slot // block
        return (target % 2) * half + (target // 2) * segment + order - target * segment

    below_row = jnp.sum((column < wide).astype(jnp.int32), axis=0, keepdims=True)
    below_column = jnp.sum((wide < column).astype(jnp.int32), axis=1, keepdims=True)
    rank_row[...] = position(row, below_row)
    rank_column = position(column, below_column)
    placed = jnp.where(rank_column == lane, column, 0)
    ordered = jnp.sum(placed, axis=0, keepdims=True).astype(F32)
    core = place[1] % 2
    mine = jnp.where(core == 0, ordered[:, :half], ordered[:, half:])
    classes, width = cot.shape
    packed[0:classes, :] = cot[...].astype(F32)
    extra = packed.shape[0] - classes
    rows = half // width
    for index in range(rows):
        packed[classes + index : classes + index + 1, :] = mine[:, index * width : (index + 1) * width]
    if extra > rows:
        packed[classes + rows :, :] = jnp.zeros((extra - rows, width), F32)


def operate(place, tile_row, tile_col, tile_count, own, near, far, tiles, field, owners):
    capacity, size, _ = tiles.shape
    count = own.shape[1] // size
    dom = place[0]
    odd = dom % 2
    near_base = (1 - odd) * 2 * count
    far_base = odd * 2 * count
    for index in range(count):
        cut = slice(index * size, (index + 1) * size)
        field[count + index] = pieces(own[:, cut])
        field[near_base + index] = pieces(near[:, cut])
        field[far_base + index] = pieces(far[:, cut])
    total = count * owners
    live = tile_count[0]
    sums = [jnp.zeros((own.shape[0], size), F32) for _ in range(count)]
    for slot in range(capacity):
        relative = lax.rem(tile_col[slot] - dom * count + count + total, total)
        target = jnp.where(slot < live, tile_row[slot], -1)
        product = whole(
            lax.dot_general(field[relative], tiles[slot], TRAILING, preferred_element_type=F32)
        )
        for index in range(count):
            sums[index] = sums[index] + jnp.where(target == index, product, 0.0)
    return jnp.concatenate(sums, axis=1)


def first_kernel(owners, place, row, col, live, own, near, far, tiles, first, field):
    first[...] = operate(place, row, col, live, own, near, far, tiles, field, owners)


def second_kernel(
    owners, place, row, col, live, own, near, far, tiles, features, rank_row, mine, other, field
):
    applied = operate(place, row, col, live, own, near, far, tiles, field, owners)
    base = features[...]
    second = 2.0 * applied - base
    diffused = series_zero * base + series_one * own[...] + series_two * second
    nodes = base.shape[1]
    spot = lax.broadcasted_iota(jnp.int32, (nodes, nodes), 0)
    chosen = jnp.where(spot == rank_row[...], 1.0, 0.0).astype(BF16)
    ordered = whole(lax.dot_general(pieces(diffused), chosen, TRAILING, preferred_element_type=F32))
    low, high = ordered[:, : nodes // 2], ordered[:, nodes // 2 :]
    core = place[1] % 2
    mine[...] = jnp.where(core == 0, low, high)
    other[...] = jnp.where(core == 0, high, low)


def cotangent_kernel(orders, classes, segment, place, *refs):
    sources = refs[: len(orders)]
    arranged, slot_rows, held, listed = refs[len(orders) :]
    me = place[0] * 2 + place[1] // 2
    core = place[1] % 2
    blocks = held.shape[0]
    width = held.shape[2]
    parts = arranged.shape[0]
    rows = listed.shape[1]
    for source, order in zip(sources, orders):
        for index, mask in enumerate(order):
            block = jnp.bitwise_xor(me, mask)
            held[block] = source[index, 0:classes, :].astype(BF16)
            listed[block] = source[index, classes : classes + rows, :]
    lists = []
    for part in range(parts):
        listing = listed[2 * part]
        row = jnp.concatenate([listing[i : i + 1] for i in range(rows)], axis=1)
        slot_rows[part] = row
        lists.append(row)
    columns = jnp.concatenate(lists, axis=0).T
    lane = lax.broadcasted_iota(jnp.int32, (segment, width), 1).astype(F32)
    for block in range(blocks):
        start = ((2 * block + core) * width).astype(F32)
        cut = slice(block * segment, (block + 1) * segment)
        chosen = jnp.concatenate(
            [
                jnp.where(columns[cut, part : part + 1] - start == lane, 1.0, 0.0)
                for part in range(parts)
            ],
            axis=0,
        ).astype(BF16)
        moved = lax.dot_general(chosen, held[block], TRAILING, preferred_element_type=F32)
        for part in range(parts):
            arranged[part, cut, :] = moved[part * segment : (part + 1) * segment].astype(BF16)


def train_kernel(counts, masks, again, place, *refs):
    sources = refs[: len(counts)]
    refs = refs[len(counts) :]
    arranged, slot_rows, w_in, w_mid, w_out = refs[:5]
    refs = refs[5:]
    if again:
        grads_before, batch_before = refs[:2]
        refs = refs[2:]
    grads, batch, held = refs
    feats = w_in.shape[0]
    classes = w_out.shape[0]
    mid_rows = grads.shape[0] - feats - arranged.shape[2]
    if again:
        grads[...] = grads_before[...]
        batch[...] = batch_before[...]
    else:
        grads[...] = jnp.zeros_like(grads)
        batch[...] = jnp.zeros_like(batch)
    slot = 0
    for source, count in zip(sources, counts):
        for index in range(count):
            held[slot] = source[index]
            slot += 1
    dom, rep = place[0], place[1]
    replicas = held.shape[1]
    width = batch.shape[1]
    own_start = (dom * replicas + rep) * width

    def one_part(step, carry):
        mask = jnp.int32(masks[0])
        for index in range(1, len(masks)):
            mask = jnp.where(step == index, masks[index], mask)
        part = jnp.bitwise_xor(dom, mask)
        value = jnp.concatenate(
            [held[step, jnp.bitwise_xor(rep, index)] for index in range(replicas)], axis=0
        )
        spot = lax.broadcasted_iota(jnp.int32, (width, value.shape[1]), 0) + own_start
        chosen = jnp.where(spot.astype(F32) == slot_rows[part], 1.0, 0.0).astype(BF16)
        batch[...] += whole(
            lax.dot_general(pieces(value), chosen, TRAILING, preferred_element_type=F32)
        )
        inputs = value.astype(BF16)
        cot = arranged[part]
        pre_one = lax.dot_general(inputs, w_in[...], LEADING, preferred_element_type=F32)
        gate_one = 0.5 * jnp.tanh(0.5 * pre_one) + 0.5
        act_one = pre_one * gate_one
        hidden_one = act_one.astype(BF16)
        slope_one = gate_one + act_one * (1.0 - gate_one)
        pre_two = jnp.dot(hidden_one, w_mid[...], preferred_element_type=F32)
        gate_two = 0.5 * jnp.tanh(0.5 * pre_two) + 0.5
        act_two = pre_two * gate_two
        hidden_two = act_two.astype(BF16)
        slope_two = gate_two + act_two * (1.0 - gate_two)
        grads[feats + mid_rows :, :] += lax.dot_general(
            cot, hidden_two, LEADING, preferred_element_type=F32
        )
        back_two = jnp.dot(cot, w_out[...], preferred_element_type=F32)
        delta_two = (back_two * slope_two).astype(BF16)
        own_pre = lax.dot_general(
            inputs,
            w_in[:, pl.ds(pl.multiple_of(dom * mid_rows, mid_rows), mid_rows)],
            LEADING,
            preferred_element_type=F32,
        )
        own_hidden = (own_pre * (0.5 * jnp.tanh(0.5 * own_pre) + 0.5)).astype(BF16)
        grads[feats : feats + mid_rows, :] += lax.dot_general(
            own_hidden, delta_two, LEADING, preferred_element_type=F32
        )
        back_one = lax.dot_general(delta_two, w_mid[...], TRAILING, preferred_element_type=F32)
        delta_one = (back_one * slope_one).astype(BF16)
        grads[0:feats, :] += jnp.dot(inputs, delta_one, preferred_element_type=F32)
        return carry

    lax.fori_loop(0, len(masks), one_part, 0)


def add_kernel(mine, theirs, grad_in, grad_mid, grad_out):
    start = 0
    for out in (grad_in, grad_mid, grad_out):
        rows = out.shape[0]
        out[...] = mine[start : start + rows, :] + theirs[start : start + rows, :]
        start += rows


def call(kernel, outs, scalars, arrays, scratch=(), cost=None, aliases=None):
    return pl.pallas_call(
        kernel,
        out_shape=outs,
        in_specs=[SMEM] * len(scalars) + [VMEM] * len(arrays),
        out_specs=jax.tree.map(lambda _: VMEM, outs),
        scratch_shapes=list(scratch),
        compiler_params=pltpu.CompilerParams(vmem_limit_bytes=48 * 2**20),
        cost_estimate=cost,
        input_output_aliases=aliases or {},
    )(*scalars, *arrays)


def exchanged(value, mask, devices):
    return lax.ppermute(value, AXES, [(i, i ^ mask) for i in range(devices)])


def gathered_plan(
    features, tiles, tile_row, tile_col, tile_count, dest_slot, w_in, w_mid, w_out, cotangent
):
    owners, replicas = lax.axis_size("dom"), lax.axis_size("rep")
    devices = owners * replicas
    place = jnp.stack([lax.axis_index("dom"), lax.axis_index("rep")]).astype(jnp.int32)
    feature_count, node_count = features.shape
    size = tiles.shape[1]
    classes, width = cotangent.shape
    hidden = w_in.shape[1]
    segment = node_count // devices
    half = node_count // 2
    count = node_count // size
    send = functools.partial(exchanged, devices=devices)
    far_pairs = [
        (d * replicas + r, ((d + 1 if d % 2 else d - 1) % owners) * replicas + r)
        for d in range(owners)
        for r in range(replicas)
    ]

    def far(value):
        return lax.ppermute(value, AXES, far_pairs)

    rows = half // width
    padded = classes + rows + (-(classes + rows)) % 8
    near_one, far_one = send(features, replicas), far(features)
    packed, rank_row = call(
        functools.partial(prepare_kernel, segment, width),
        (
            jax.ShapeDtypeStruct((padded, width), F32),
            jax.ShapeDtypeStruct((1, node_count), jnp.int32),
        ),
        [place],
        [dest_slot.reshape(1, -1), cotangent],
    )
    field = pltpu.VMEM((3 * count, 3 * feature_count, size), BF16)
    scalars = [place, tile_row, tile_col, tile_count]
    first = call(
        functools.partial(first_kernel, owners),
        jax.ShapeDtypeStruct(features.shape, F32),
        scalars,
        [features, near_one, far_one, tiles],
        [field],
    )
    line = [packed] + [send(packed, m) for m in (8, 16, 24)]
    column = jnp.stack(line)
    near_two, far_two = send(first, replicas), far(first)
    across_x, across_y = send(column, 4), send(column, 2)
    corner_one, corner_two = send(across_y[0:2], 4), send(across_x[2:4], 2)
    mine, other = call(
        functools.partial(second_kernel, owners),
        tuple(jax.ShapeDtypeStruct((feature_count, half), F32) for _ in range(2)),
        scalars,
        [first, near_two, far_two, tiles, features, rank_row],
        [field],
    )
    own = jnp.stack([mine, send(other, 1), send(mine, 2), send(other, 3)])
    parts = {0: own[None]}
    parts[1] = send(own, 4)[None]
    ring = [send(own, m) for m in (8, 16, 24)]
    last = send(jnp.stack(ring), 4)
    orders = ((0, 4, 8, 12), (2, 6, 10, 14), (1, 5, 9, 13), (3, 7), (11, 15))
    arranged, slot_rows = call(
        functools.partial(cotangent_kernel, orders, classes, segment),
        (
            jax.ShapeDtypeStruct((owners, half, classes), BF16),
            jax.ShapeDtypeStruct((owners, 1, half), F32),
        ),
        [place],
        [column, across_x, across_y, corner_one, corner_two],
        [
            pltpu.VMEM((devices // 2, classes, width), BF16),
            pltpu.VMEM((devices // 2, rows, width), F32),
        ],
    )
    mid_rows = hidden // owners
    total_rows = feature_count * replicas + mid_rows + classes

    def train(sources, masks, before=()):
        counts = tuple(s.shape[0] for s in sources)
        inputs = [*sources, arranged, slot_rows, w_in, w_mid, w_out, *before]
        return call(
            functools.partial(train_kernel, counts, masks, bool(before)),
            (
                jax.ShapeDtypeStruct((total_rows, hidden), F32),
                jax.ShapeDtypeStruct((feature_count * replicas, width), F32),
            ),
            [place],
            inputs,
            [pltpu.VMEM((len(masks), replicas, feature_count, half), F32)],
            pl.CostEstimate(
                flops=5_800_000 * half * len(masks), bytes_accessed=8 * 2**20, transcendentals=0
            ),
        )

    state = train([parts[0], parts[1]], (0, 1))
    state = train([r[None] for r in ring], (2, 4, 6), state)
    grads, batch_features = train([last], (3, 5, 7), state)
    grad_in, grad_mid, grad_out = call(
        add_kernel,
        tuple(
            jax.ShapeDtypeStruct((n, hidden), F32)
            for n in (feature_count * replicas, mid_rows, classes)
        ),
        [],
        [grads, send(grads, 1)],
    )
    return batch_features, grad_in, grad_mid, grad_out


def extended_2(cells, sides, width):
    for axis, dim in sides:
        count = lax.axis_size(axis)
        head = lax.slice_in_dim(cells, 0, width, axis=dim)
        tail = lax.slice_in_dim(cells, cells.shape[dim] - width, cells.shape[dim], axis=dim)
        cells = jnp.concatenate(
            [
                lax.ppermute(tail, axis, [(i, (i + 1) % count) for i in range(count)]),
                cells,
                lax.ppermute(head, axis, [((i + 1) % count, i) for i in range(count)]),
            ],
            axis=dim,
        )
    return cells


def silu_slope(pre):
    sigma = jax.nn.sigmoid(pre)
    return sigma * (1.0 + pre * (1.0 - sigma))


def neighbour_blocks(local, margin, tile_size):
    extended = extended_2(local, (("dom", 1),), margin * tile_size)
    return extended


def apply_operator(local, tiles_across, assignment_map, relative, margin):
    feature_count, node_count = local.shape
    tile_size = tiles_across.shape[1]
    extended = neighbour_blocks(local, margin, tile_size)
    blocks = extended.reshape(feature_count, -1, tile_size)
    input_values = jnp.take(blocks, relative, axis=1)
    block_products = jnp.einsum(
        "lkz,glz->glk", tiles_across, input_values, precision=lax.Precision.HIGHEST
    )
    final_result = jnp.einsum(
        "wy,kya->kwa", assignment_map, block_products, precision=lax.Precision.HIGHEST
    )
    return final_result.reshape(feature_count, node_count)


def split_plan(
    features, tiles, tile_row, tile_col, tile_count, dest_slot, w_in, w_mid, w_out, cotangent
):
    node_partition = lax.axis_index("dom")
    owners = lax.axis_size("dom")
    replicas = lax.axis_size("rep")
    feature_count, node_count = features.shape
    capacity = tiles.shape[0]
    tile_size = tiles.shape[1]
    block_count = node_count // tile_size
    total_blocks = block_count * owners
    relative = jnp.mod(tile_col - node_partition * block_count + block_count, total_blocks)
    live_mask = (jnp.arange(capacity, dtype=jnp.int32) < tile_count[0]).astype(jnp.float32)
    assignment_map = (
        tile_row[None, :] == jnp.arange(block_count, dtype=jnp.int32)[:, None]
    ).astype(jnp.float32) * live_mask[None, :]
    tiles_across = tiles.astype(jnp.float32)
    first = apply_operator(features, tiles_across, assignment_map, relative, block_count)
    second = (
        2.0 * apply_operator(first, tiles_across, assignment_map, relative, block_count) - features
    )
    diffused = series_zero * features + series_one * first + series_two * second
    segment = node_count // (owners * replicas)
    batch_rows = node_count // replicas
    sort_order = jnp.argsort(dest_slot)
    sorted_slots = jnp.take(dest_slot, sort_order)
    moved_rows = jnp.take(diffused, sort_order, axis=1).reshape(
        feature_count, owners, replicas, segment
    )
    moved_slots = sorted_slots.astype(jnp.float32).reshape(1, owners, replicas, segment)
    arrived, arrived_slots = (
        lax.all_to_all(
            lax.all_to_all(moved_rows, "dom", split_axis=1, concat_axis=1, tiled=True),
            "rep",
            split_axis=2,
            concat_axis=0,
            tiled=True,
        ),
        lax.all_to_all(
            lax.all_to_all(moved_slots, "dom", split_axis=1, concat_axis=1, tiled=True),
            "rep",
            split_axis=2,
            concat_axis=0,
            tiled=True,
        ),
    )
    owner_index = node_partition * replicas + lax.axis_index("rep")
    local_slots = arrived_slots[0].reshape(-1).astype(jnp.int32) - owner_index * batch_rows
    gathered = arrived.reshape(feature_count * replicas, -1)
    batch_features = jnp.zeros(gathered.shape, jnp.float32).at[:, local_slots].set(gathered)
    inputs_bf = batch_features.astype(jnp.bfloat16)
    pre_one = lax.dot_general(inputs_bf, w_in, LEADING, preferred_element_type=jnp.float32)
    hidden_one = jax.nn.silu(pre_one).astype(jnp.bfloat16)
    pre_two = jnp.dot(hidden_one, w_mid, preferred_element_type=jnp.float32)
    hidden_two = jax.nn.silu(pre_two).astype(jnp.bfloat16)
    grad_out = jnp.dot(cotangent, hidden_two, preferred_element_type=jnp.float32)
    back_two = lax.dot_general(cotangent, w_out, LEADING, preferred_element_type=jnp.float32)
    delta_two = (back_two * silu_slope(pre_two)).astype(jnp.bfloat16)
    back_one = lax.dot_general(delta_two, w_mid, TRAILING, preferred_element_type=jnp.float32)
    delta_one = (back_one * silu_slope(pre_one)).astype(jnp.bfloat16)
    grad_in = jnp.dot(inputs_bf, delta_one, preferred_element_type=jnp.float32)
    mid_shard = lax.psum_scatter(
        lax.dot_general(hidden_one, delta_two, LEADING, preferred_element_type=jnp.float32),
        "dom",
        scatter_dimension=0,
        tiled=True,
    )
    grad_mid = lax.psum(mid_shard, "rep")
    grad_in, grad_out = lax.psum((grad_in, grad_out), ("dom", "rep"))
    return (batch_features, grad_in, grad_mid, grad_out)


def solution(mesh):
    compact = mesh.shape["dom"] == 8 and mesh.shape["rep"] == 4
    shards = gathered_plan if compact else split_plan
    in_specs = (
        P("rep", "dom"),
        P("dom", None, None),
        P("dom"),
        P("dom"),
        P("dom"),
        P("dom"),
        P(),
        P(),
        P(),
        P(None, ("dom", "rep")),
    )
    out_specs = (P(None, ("dom", "rep")), P(), P("dom", None), P())
    return jax.shard_map(shards, mesh=mesh, in_specs=in_specs, out_specs=out_specs, check_vma=False)
```

```python
import functools

import jax
import jax.numpy as jnp
from jax import lax
from jax.experimental import pallas as pl
from jax.experimental.pallas import tpu as pltpu
from jax.sharding import PartitionSpec as P

series_zero = 0.3085083
series_one = -0.4305395
series_two = 0.1864784
LEADING = (((0,), (0,)), ((), ()))
TRAILING = (((1,), (1,)), ((), ()))
AXES = ("dom", "rep")
F32 = jnp.float32
BF16 = jnp.bfloat16
VMEM = pl.BlockSpec(memory_space=pltpu.VMEM)
SMEM = pl.BlockSpec(memory_space=pltpu.SMEM)


def pieces(value):
    high = value.astype(BF16)
    rest = value - high.astype(F32)
    middle = rest.astype(BF16)
    low = (rest - middle.astype(F32)).astype(BF16)
    return jnp.concatenate([high, middle, low], axis=0)


def whole(parts):
    rows = parts.shape[0] // 3
    return parts[:rows] + parts[rows : 2 * rows] + parts[2 * rows :]


def prepare_kernel(segment, block, place, slots_hbm, cot_hbm, packed, rank_row, slots, cot, sems):
    fetch_slots = pltpu.make_async_copy(slots_hbm, slots, sems.at[0])
    fetch_cot = pltpu.make_async_copy(cot_hbm, cot, sems.at[1])
    fetch_slots.start()
    fetch_cot.start()
    fetch_slots.wait()
    nodes = slots.shape[1]
    half = nodes // 2
    row = slots[...].astype(F32)
    column = jnp.broadcast_to(row, (8, nodes)).T[:, 0:1]
    wide = jnp.broadcast_to(row, (nodes, nodes))
    order = jnp.sum(jnp.where(column < wide, 1.0, 0.0), axis=0, keepdims=True).astype(jnp.int32)
    target = slots[...] // block
    rank = (target % 2) * half + (target // 2) * segment + order - target * segment
    rank_row[...] = rank
    rank_column = jnp.broadcast_to(rank.astype(F32), (8, nodes)).T[:, 0:1]
    lane = lax.broadcasted_iota(jnp.int32, (nodes, nodes), 1).astype(F32)
    ordered = jnp.sum(jnp.where(rank_column == lane, column, 0.0), axis=0, keepdims=True)
    mine = jnp.where(place[1] % 2 == 0, ordered[:, :half], ordered[:, half:])
    classes, width = cot.shape
    fetch_cot.wait()
    packed[0:classes, :] = cot[...].astype(F32)
    extra = packed.shape[0] - classes
    rows = half // width
    for index in range(rows):
        packed[classes + index : classes + index + 1, :] = mine[:, index * width : (index + 1) * width]
    if extra > rows:
        packed[classes + rows :, :] = jnp.zeros((extra - rows, width), F32)


def operate(place, live, row, col, own, near, far, tiles, field, owners):
    capacity, size, _ = tiles.shape
    count = own.shape[1] // size
    dom = place[0]
    odd = dom % 2
    near_base = (1 - odd) * 2 * count
    far_base = odd * 2 * count
    for index in range(count):
        cut = slice(index * size, (index + 1) * size)
        field[count + index] = pieces(own[:, cut])
        field[near_base + index] = pieces(near[:, cut])
        field[far_base + index] = pieces(far[:, cut])
    total = count * owners
    sums = [jnp.zeros((own.shape[0], size), F32) for _ in range(count)]
    for slot in range(capacity):
        relative = lax.rem(col[slot] - dom * count + count + total, total)
        target = jnp.where(slot < live[0], row[slot], -1)
        product = whole(
            lax.dot_general(field[relative], tiles[slot], TRAILING, preferred_element_type=F32)
        )
        for index in range(count):
            sums[index] = sums[index] + jnp.where(target == index, product, 0.0)
    return jnp.concatenate(sums, axis=1)


def first_kernel(owners, place, live, row, col, own, near, far, tiles, first, field):
    first[...] = operate(place, live, row, col, own, near, far, tiles, field, owners)


def second_kernel(
    owners, place, live, row, col, own, near, far, tiles, features, rank_row, mine, other, field
):
    applied = operate(place, live, row, col, own, near, far, tiles, field, owners)
    base = features[...]
    second = 2.0 * applied - base
    diffused = series_zero * base + series_one * own[...] + series_two * second
    nodes = base.shape[1]
    spot = lax.broadcasted_iota(jnp.int32, (nodes, nodes), 0)
    chosen = jnp.where(spot == rank_row[...], 1.0, 0.0).astype(BF16)
    ordered = whole(lax.dot_general(pieces(diffused), chosen, TRAILING, preferred_element_type=F32))
    low, high = ordered[:, : nodes // 2], ordered[:, nodes // 2 :]
    core = place[1] % 2
    mine[...] = jnp.where(core == 0, low, high)
    other[...] = jnp.where(core == 0, high, low)


def cotangent_kernel(orders, classes, segment, place, *refs):
    sources = refs[: len(orders)]
    arranged, slot_rows, held, listed = refs[len(orders) :]
    me = place[0] * 2 + place[1] // 2
    core = place[1] % 2
    blocks = held.shape[0]
    width = held.shape[2]
    parts = arranged.shape[0]
    rows = listed.shape[1]
    for source, order in zip(sources, orders):
        for index, mask in enumerate(order):
            block = jnp.bitwise_xor(me, mask)
            held[block] = source[index, 0:classes, :].astype(BF16)
            listed[block] = source[index, classes : classes + rows, :]
    lists = []
    for part in range(parts):
        listing = listed[2 * part]
        row = jnp.concatenate([listing[i : i + 1] for i in range(rows)], axis=1)
        slot_rows[part] = row
        lists.append(row)
    columns = jnp.concatenate(lists, axis=0).T
    lane = lax.broadcasted_iota(jnp.int32, (segment, width), 1).astype(F32)
    for block in range(blocks):
        start = ((2 * block + core) * width).astype(F32)
        cut = slice(block * segment, (block + 1) * segment)
        chosen = jnp.concatenate(
            [
                jnp.where(columns[cut, part : part + 1] - start == lane, 1.0, 0.0)
                for part in range(parts)
            ],
            axis=0,
        ).astype(BF16)
        moved = lax.dot_general(chosen, held[block], TRAILING, preferred_element_type=F32)
        for part in range(parts):
            arranged[part, cut, :] = moved[part * segment : (part + 1) * segment].astype(BF16)


def activated(pre):
    gate = 0.5 * jnp.tanh(0.5 * pre) + 0.5
    value = pre * gate
    return value.astype(BF16), gate + value * (1.0 - gate)


def feature_rows(source, rep):
    replicas = source.shape[0]
    return jnp.concatenate([source[jnp.bitwise_xor(rep, i)] for i in range(replicas)], axis=0)


def forward(inputs, dom, mid_rows, w_in, w_mid):
    pre_one = lax.dot_general(inputs, w_in[...], LEADING, preferred_element_type=F32)
    hidden_one, slope_one = activated(pre_one)
    own_pre = lax.dot_general(
        inputs,
        w_in[:, pl.ds(pl.multiple_of(dom * mid_rows, mid_rows), mid_rows)],
        LEADING,
        preferred_element_type=F32,
    )
    own_hidden, _ = activated(own_pre)
    pre_two = jnp.dot(hidden_one, w_mid[...], preferred_element_type=F32)
    hidden_two, slope_two = activated(pre_two)
    return own_hidden, hidden_two, slope_one, slope_two


def forward_kernel(mid_rows, place, *refs):
    *sources, w_in, w_mid, own_hidden, hidden_two, slope_one, slope_two = refs
    dom, rep = place[0], place[1]
    values = [feature_rows(source, rep).astype(BF16) for source in sources]
    results = forward(jnp.concatenate(values, axis=1), dom, mid_rows, w_in, w_mid)
    for out, result in zip((own_hidden, hidden_two, slope_one, slope_two), results):
        out[...] = result


def train_kernel(fresh, masks, begun, again, place, *refs):
    if again:
        grads_before, batch_before = refs[:2]
        refs = refs[2:]
    sources = refs[: len(masks)]
    refs = refs[len(masks) :]
    states = refs[:4] if begun else ()
    arranged, slot_rows, w_in, w_mid, w_out, grads, batch = refs[len(states) :]
    feats = w_in.shape[0]
    mid_rows = grads.shape[0] - feats - arranged.shape[2]
    dom, rep = place[0], place[1]
    width = batch.shape[1]
    replicas = sources[0].shape[0]
    own_start = (dom * replicas + rep) * width
    values, cots = [], []
    moved = batch_before[...] if again else jnp.zeros(batch.shape, F32)
    for source, mask in zip(sources, masks):
        part = jnp.bitwise_xor(dom, mask)
        value = feature_rows(source, rep)
        spot = lax.broadcasted_iota(jnp.int32, (width, value.shape[1]), 0) + own_start
        chosen = jnp.where(spot.astype(F32) == slot_rows[part], 1.0, 0.0).astype(BF16)
        moved = moved + whole(
            lax.dot_general(pieces(value), chosen, TRAILING, preferred_element_type=F32)
        )
        values.append(value.astype(BF16))
        cots.append(arranged[part])
    batch[...] = moved
    inputs = jnp.concatenate(values, axis=1)
    cot = jnp.concatenate(cots, axis=0)
    done = inputs.shape[1] - fresh
    results = forward(inputs[:, done:], dom, mid_rows, w_in, w_mid)
    if begun:
        results = [
            jnp.concatenate([state[...], result], axis=0) for state, result in zip(states, results)
        ]
    own_hidden, hidden_two, slope_one, slope_two = results

    def add(first_row, last_row, term):
        cut = slice(first_row, last_row)
        grads[cut, :] = grads_before[cut, :] + term if again else term

    add(
        feats + mid_rows,
        grads.shape[0],
        lax.dot_general(cot, hidden_two, LEADING, preferred_element_type=F32),
    )
    back_two = jnp.dot(cot, w_out[...], preferred_element_type=F32)
    delta_two = (back_two * slope_two).astype(BF16)
    add(
        feats,
        feats + mid_rows,
        lax.dot_general(own_hidden, delta_two, LEADING, preferred_element_type=F32),
    )
    back_one = lax.dot_general(delta_two, w_mid[...], TRAILING, preferred_element_type=F32)
    delta_one = (back_one * slope_one).astype(BF16)
    add(0, feats, jnp.dot(inputs, delta_one, preferred_element_type=F32))


def add_kernel(mine, theirs, grad_in, grad_mid, grad_out):
    start = 0
    for out in (grad_in, grad_mid, grad_out):
        rows = out.shape[0]
        out[...] = mine[start : start + rows, :] + theirs[start : start + rows, :]
        start += rows


def call(kernel, outs, scalars, arrays, scratch=(), micros=1.5, space=pltpu.VMEM):
    cost = pl.CostEstimate(
        flops=int(micros * 1e9), bytes_accessed=int(micros * 3.6e6), transcendentals=0
    )
    return pl.pallas_call(
        kernel,
        out_shape=outs,
        in_specs=[SMEM] * len(scalars) + [pl.BlockSpec(memory_space=space)] * len(arrays),
        out_specs=jax.tree.map(lambda _: VMEM, outs),
        scratch_shapes=list(scratch),
        compiler_params=pltpu.CompilerParams(vmem_limit_bytes=48 * 2**20),
        cost_estimate=cost,
    )(*scalars, *arrays)


def exchanged(value, mask, devices):
    return lax.ppermute(value, AXES, [(i, i ^ mask) for i in range(devices)])


def gathered_plan(
    features, tiles, tile_row, tile_col, tile_count, dest_slot, w_in, w_mid, w_out, cotangent
):
    owners, replicas = lax.axis_size("dom"), lax.axis_size("rep")
    devices = owners * replicas
    place = jnp.stack([lax.axis_index("dom"), lax.axis_index("rep")]).astype(jnp.int32)
    scalars = [place, tile_count, tile_row, tile_col]
    feature_count, node_count = features.shape
    size = tiles.shape[1]
    classes, width = cotangent.shape
    hidden = w_in.shape[1]
    segment = node_count // devices
    half = node_count // 2
    count = node_count // size
    send = functools.partial(exchanged, devices=devices)
    far_pairs = [
        (d * replicas + r, ((d + 1 if d % 2 else d - 1) % owners) * replicas + r)
        for d in range(owners)
        for r in range(replicas)
    ]

    def far(value):
        return lax.ppermute(value, AXES, far_pairs)

    rows = half // width
    padded = classes + rows + (-(classes + rows)) % 8
    near_one, far_one = send(features, replicas), far(features)
    packed, rank_row = call(
        functools.partial(prepare_kernel, segment, width),
        (
            jax.ShapeDtypeStruct((padded, width), F32),
            jax.ShapeDtypeStruct((1, node_count), jnp.int32),
        ),
        [place],
        [dest_slot.reshape(1, -1), cotangent],
        [
            pltpu.VMEM((1, node_count), jnp.int32),
            pltpu.VMEM((classes, width), BF16),
            pltpu.SemaphoreType.DMA((2,)),
        ],
        space=pl.ANY,
    )
    field = pltpu.VMEM((3 * count, 3 * feature_count, size), BF16)
    first = call(
        functools.partial(first_kernel, owners),
        jax.ShapeDtypeStruct(features.shape, F32),
        scalars,
        [features, near_one, far_one, tiles],
        [field],
    )
    line = [packed] + [send(packed, m) for m in (8, 16, 24)]
    column = jnp.stack(line)
    near_two, far_two = send(first, replicas), far(first)
    across_x, across_y = send(column, 4), send(column, 2)
    corner_one, corner_two = send(across_y[0:2], 4), send(across_x[2:4], 2)
    mine, other = call(
        functools.partial(second_kernel, owners),
        tuple(jax.ShapeDtypeStruct((feature_count, half), F32) for _ in range(2)),
        scalars,
        [first, near_two, far_two, tiles, features, rank_row],
        [field],
    )
    own = jnp.stack([mine, send(other, 1), send(mine, 2), send(other, 3)])
    facing = send(own, 4)
    ring = [send(own, m) for m in (8, 16, 24)]
    orders = ((0, 4, 8, 12), (2, 6, 10, 14), (1, 5, 9, 13), (3, 7), (11, 15))
    arranged, slot_rows = call(
        functools.partial(cotangent_kernel, orders, classes, segment),
        (
            jax.ShapeDtypeStruct((owners, half, classes), BF16),
            jax.ShapeDtypeStruct((owners, 1, half), F32),
        ),
        [place],
        [column, across_x, across_y, corner_one, corner_two],
        [
            pltpu.VMEM((devices // 2, classes, width), BF16),
            pltpu.VMEM((devices // 2, rows, width), F32),
        ],
    )
    mid_rows = hidden // owners
    total_rows = feature_count * replicas + mid_rows + classes

    begun = call(
        functools.partial(forward_kernel, mid_rows),
        (
            jax.ShapeDtypeStruct((2 * half, mid_rows), BF16),
            jax.ShapeDtypeStruct((2 * half, hidden), BF16),
            jax.ShapeDtypeStruct((2 * half, hidden), F32),
            jax.ShapeDtypeStruct((2 * half, hidden), F32),
        ),
        [place],
        [own, facing, w_in, w_mid],
        micros=2.5,
    )
    *ring, gate = lax.optimization_barrier((*ring, begun[0]))
    begun = (gate, *begun[1:])
    last = send(jnp.stack(ring), 4)

    def train(before, sources, masks, states):
        fresh = half * (len(masks) - 2 * bool(states))
        return call(
            functools.partial(train_kernel, fresh, masks, bool(states), bool(before)),
            (
                jax.ShapeDtypeStruct((total_rows, hidden), F32),
                jax.ShapeDtypeStruct((feature_count * replicas, width), F32),
            ),
            [place],
            [*before, *sources, *states, arranged, slot_rows, w_in, w_mid, w_out],
            micros=2.5 * len(masks),
        )

    state = train((), [own, facing, *ring], (0, 1, 2, 4, 6), begun)
    grads, batch_features = train(state, [last[0], last[1], last[2]], (3, 5, 7), ())
    grad_in, grad_mid, grad_out = call(
        add_kernel,
        tuple(
            jax.ShapeDtypeStruct((n, hidden), F32)
            for n in (feature_count * replicas, mid_rows, classes)
        ),
        [],
        [grads, send(grads, 1)],
    )
    return batch_features, grad_in, grad_mid, grad_out


def extended_2(cells, sides, width):
    for axis, dim in sides:
        count = lax.axis_size(axis)
        head = lax.slice_in_dim(cells, 0, width, axis=dim)
        tail = lax.slice_in_dim(cells, cells.shape[dim] - width, cells.shape[dim], axis=dim)
        cells = jnp.concatenate(
            [
                lax.ppermute(tail, axis, [(i, (i + 1) % count) for i in range(count)]),
                cells,
                lax.ppermute(head, axis, [((i + 1) % count, i) for i in range(count)]),
            ],
            axis=dim,
        )
    return cells


def silu_slope(pre):
    sigma = jax.nn.sigmoid(pre)
    return sigma * (1.0 + pre * (1.0 - sigma))


def neighbour_blocks(local, margin, tile_size):
    extended = extended_2(local, (("dom", 1),), margin * tile_size)
    return extended


def apply_operator(local, tiles_across, assignment_map, relative, margin):
    feature_count, node_count = local.shape
    tile_size = tiles_across.shape[1]
    extended = neighbour_blocks(local, margin, tile_size)
    blocks = extended.reshape(feature_count, -1, tile_size)
    input_values = jnp.take(blocks, relative, axis=1)
    block_products = jnp.einsum(
        "lkz,glz->glk", tiles_across, input_values, precision=lax.Precision.HIGHEST
    )
    final_result = jnp.einsum(
        "wy,kya->kwa", assignment_map, block_products, precision=lax.Precision.HIGHEST
    )
    return final_result.reshape(feature_count, node_count)


def split_plan(
    features, tiles, tile_row, tile_col, tile_count, dest_slot, w_in, w_mid, w_out, cotangent
):
    node_partition = lax.axis_index("dom")
    owners = lax.axis_size("dom")
    replicas = lax.axis_size("rep")
    feature_count, node_count = features.shape
    capacity = tiles.shape[0]
    tile_size = tiles.shape[1]
    block_count = node_count // tile_size
    total_blocks = block_count * owners
    relative = jnp.mod(tile_col - node_partition * block_count + block_count, total_blocks)
    live_mask = (jnp.arange(capacity, dtype=jnp.int32) < tile_count[0]).astype(jnp.float32)
    assignment_map = (
        tile_row[None, :] == jnp.arange(block_count, dtype=jnp.int32)[:, None]
    ).astype(jnp.float32) * live_mask[None, :]
    tiles_across = tiles.astype(jnp.float32)
    first = apply_operator(features, tiles_across, assignment_map, relative, block_count)
    second = (
        2.0 * apply_operator(first, tiles_across, assignment_map, relative, block_count) - features
    )
    diffused = series_zero * features + series_one * first + series_two * second
    segment = node_count // (owners * replicas)
    batch_rows = node_count // replicas
    sort_order = jnp.argsort(dest_slot)
    sorted_slots = jnp.take(dest_slot, sort_order)
    moved_rows = jnp.take(diffused, sort_order, axis=1).reshape(
        feature_count, owners, replicas, segment
    )
    moved_slots = sorted_slots.astype(jnp.float32).reshape(1, owners, replicas, segment)
    arrived, arrived_slots = (
        lax.all_to_all(
            lax.all_to_all(moved_rows, "dom", split_axis=1, concat_axis=1, tiled=True),
            "rep",
            split_axis=2,
            concat_axis=0,
            tiled=True,
        ),
        lax.all_to_all(
            lax.all_to_all(moved_slots, "dom", split_axis=1, concat_axis=1, tiled=True),
            "rep",
            split_axis=2,
            concat_axis=0,
            tiled=True,
        ),
    )
    owner_index = node_partition * replicas + lax.axis_index("rep")
    local_slots = arrived_slots[0].reshape(-1).astype(jnp.int32) - owner_index * batch_rows
    gathered = arrived.reshape(feature_count * replicas, -1)
    batch_features = jnp.zeros(gathered.shape, jnp.float32).at[:, local_slots].set(gathered)
    inputs_bf = batch_features.astype(jnp.bfloat16)
    pre_one = lax.dot_general(inputs_bf, w_in, LEADING, preferred_element_type=jnp.float32)
    hidden_one = jax.nn.silu(pre_one).astype(jnp.bfloat16)
    pre_two = jnp.dot(hidden_one, w_mid, preferred_element_type=jnp.float32)
    hidden_two = jax.nn.silu(pre_two).astype(jnp.bfloat16)
    grad_out = jnp.dot(cotangent, hidden_two, preferred_element_type=jnp.float32)
    back_two = lax.dot_general(cotangent, w_out, LEADING, preferred_element_type=jnp.float32)
    delta_two = (back_two * silu_slope(pre_two)).astype(jnp.bfloat16)
    back_one = lax.dot_general(delta_two, w_mid, TRAILING, preferred_element_type=jnp.float32)
    delta_one = (back_one * silu_slope(pre_one)).astype(jnp.bfloat16)
    grad_in = jnp.dot(inputs_bf, delta_one, preferred_element_type=jnp.float32)
    mid_shard = lax.psum_scatter(
        lax.dot_general(hidden_one, delta_two, LEADING, preferred_element_type=jnp.float32),
        "dom",
        scatter_dimension=0,
        tiled=True,
    )
    grad_mid = lax.psum(mid_shard, "rep")
    grad_in, grad_out = lax.psum((grad_in, grad_out), ("dom", "rep"))
    return (batch_features, grad_in, grad_mid, grad_out)


def solution(mesh):
    compact = mesh.shape["dom"] == 8 and mesh.shape["rep"] == 4
    shards = gathered_plan if compact else split_plan
    in_specs = (
        P("rep", "dom"),
        P("dom", None, None),
        P("dom"),
        P("dom"),
        P("dom"),
        P("dom"),
        P(),
        P(),
        P(),
        P(None, ("dom", "rep")),
    )
    out_specs = (P(None, ("dom", "rep")), P(), P("dom", None), P())
    return jax.shard_map(shards, mesh=mesh, in_specs=in_specs, out_specs=out_specs, check_vma=False)
```

```python
import functools

import jax
import jax.numpy as jnp
from jax import lax
from jax.experimental import pallas as pl
from jax.experimental.pallas import tpu as pltpu
from jax.sharding import PartitionSpec as P

series_zero = 0.3085083
series_one = -0.4305395
series_two = 0.1864784
LEADING = (((0,), (0,)), ((), ()))
TRAILING = (((1,), (1,)), ((), ()))
AXES = ("dom", "rep")
F32 = jnp.float32
BF16 = jnp.bfloat16
VMEM = pl.BlockSpec(memory_space=pltpu.VMEM)
SMEM = pl.BlockSpec(memory_space=pltpu.SMEM)


def pieces(value):
    high = value.astype(BF16)
    rest = value - high.astype(F32)
    middle = rest.astype(BF16)
    low = (rest - middle.astype(F32)).astype(BF16)
    return jnp.concatenate([high, middle, low], axis=0)


def whole(parts):
    rows = parts.shape[0] // 3
    return parts[:rows] + parts[rows : 2 * rows] + parts[2 * rows :]


def prepare_kernel(segment, block, place, slots_hbm, cot_hbm, packed, rank_row, slots, cot, sems):
    fetch_slots = pltpu.make_async_copy(slots_hbm, slots, sems.at[0])
    fetch_cot = pltpu.make_async_copy(cot_hbm, cot, sems.at[1])
    fetch_slots.start()
    fetch_cot.start()
    fetch_slots.wait()
    nodes = slots.shape[1]
    half = nodes // 2
    row = slots[...].astype(F32)
    column = jnp.broadcast_to(row, (8, nodes)).T[:, 0:1]
    wide = jnp.broadcast_to(row, (nodes, nodes))
    order = jnp.sum(jnp.where(column < wide, 1.0, 0.0), axis=0, keepdims=True).astype(jnp.int32)
    target = slots[...] // block
    rank = (target % 2) * half + (target // 2) * segment + order - target * segment
    rank_row[...] = rank
    rank_column = jnp.broadcast_to(rank.astype(F32), (8, nodes)).T[:, 0:1]
    lane = lax.broadcasted_iota(jnp.int32, (nodes, nodes), 1).astype(F32)
    ordered = jnp.sum(jnp.where(rank_column == lane, column, 0.0), axis=0, keepdims=True)
    mine = jnp.where(place[1] % 2 == 0, ordered[:, :half], ordered[:, half:])
    classes, width = cot.shape
    fetch_cot.wait()
    packed[0:classes, :] = cot[...].astype(F32)
    extra = packed.shape[0] - classes
    rows = half // width
    for index in range(rows):
        packed[classes + index : classes + index + 1, :] = mine[:, index * width : (index + 1) * width]
    if extra > rows:
        packed[classes + rows :, :] = jnp.zeros((extra - rows, width), F32)


def operate(place, live, row, col, own, near, far, tiles, field, owners):
    capacity, size, _ = tiles.shape
    count = own.shape[1] // size
    dom = place[0]
    odd = dom % 2
    near_base = (1 - odd) * 2 * count
    far_base = odd * 2 * count
    for index in range(count):
        cut = slice(index * size, (index + 1) * size)
        field[count + index] = pieces(own[:, cut])
        field[near_base + index] = pieces(near[:, cut])
        field[far_base + index] = pieces(far[:, cut])
    total = count * owners
    sums = [jnp.zeros((own.shape[0], size), F32) for _ in range(count)]
    for slot in range(capacity):
        relative = lax.rem(col[slot] - dom * count + count + total, total)
        target = jnp.where(slot < live[0], row[slot], -1)
        product = whole(
            lax.dot_general(field[relative], tiles[slot], TRAILING, preferred_element_type=F32)
        )
        for index in range(count):
            sums[index] = sums[index] + jnp.where(target == index, product, 0.0)
    return jnp.concatenate(sums, axis=1)


def first_kernel(owners, place, live, row, col, own, near, far, tiles, first, field):
    first[...] = operate(place, live, row, col, own, near, far, tiles, field, owners)


def second_kernel(
    owners, place, live, row, col, own, near, far, tiles, features, rank_row, mine, other, field
):
    applied = operate(place, live, row, col, own, near, far, tiles, field, owners)
    base = features[...]
    second = 2.0 * applied - base
    diffused = series_zero * base + series_one * own[...] + series_two * second
    nodes = base.shape[1]
    spot = lax.broadcasted_iota(jnp.int32, (nodes, nodes), 0)
    chosen = jnp.where(spot == rank_row[...], 1.0, 0.0).astype(BF16)
    ordered = whole(lax.dot_general(pieces(diffused), chosen, TRAILING, preferred_element_type=F32))
    low, high = ordered[:, : nodes // 2], ordered[:, nodes // 2 :]
    core = place[1] % 2
    mine[...] = jnp.where(core == 0, low, high)
    other[...] = jnp.where(core == 0, high, low)


def cotangent_kernel(orders, classes, segment, place, *refs):
    sources = refs[: len(orders)]
    arranged, slot_rows, held, listed = refs[len(orders) :]
    me = place[0] * 2 + place[1] // 2
    core = place[1] % 2
    blocks = held.shape[0]
    width = held.shape[2]
    parts = arranged.shape[0]
    rows = listed.shape[1]
    for source, order in zip(sources, orders):
        for index, mask in enumerate(order):
            block = jnp.bitwise_xor(me, mask)
            held[block] = source[index, 0:classes, :].astype(BF16)
            listed[block] = source[index, classes : classes + rows, :]
    lists = []
    for part in range(parts):
        listing = listed[2 * part]
        row = jnp.concatenate([listing[i : i + 1] for i in range(rows)], axis=1)
        slot_rows[part] = row
        lists.append(row)
    columns = jnp.concatenate(lists, axis=0).T
    lane = lax.broadcasted_iota(jnp.int32, (segment, width), 1).astype(F32)
    for block in range(blocks):
        start = ((2 * block + core) * width).astype(F32)
        cut = slice(block * segment, (block + 1) * segment)
        chosen = jnp.concatenate(
            [
                jnp.where(columns[cut, part : part + 1] - start == lane, 1.0, 0.0)
                for part in range(parts)
            ],
            axis=0,
        ).astype(BF16)
        moved = lax.dot_general(chosen, held[block], TRAILING, preferred_element_type=F32)
        for part in range(parts):
            arranged[part, cut, :] = moved[part * segment : (part + 1) * segment].astype(BF16)


def activated(pre):
    gate = 0.5 * jnp.tanh(0.5 * pre) + 0.5
    value = pre * gate
    return value.astype(BF16), gate + value * (1.0 - gate)


def feature_rows(source, rep):
    replicas = source.shape[0]
    return jnp.concatenate([source[jnp.bitwise_xor(rep, i)] for i in range(replicas)], axis=0)


def forward(inputs, dom, mid_rows, w_in, w_mid):
    pre_one = lax.dot_general(inputs, w_in[...], LEADING, preferred_element_type=F32)
    hidden_one, slope_one = activated(pre_one)
    own_pre = lax.dot_general(
        inputs,
        w_in[:, pl.ds(pl.multiple_of(dom * mid_rows, mid_rows), mid_rows)],
        LEADING,
        preferred_element_type=F32,
    )
    own_hidden, _ = activated(own_pre)
    pre_two = jnp.dot(hidden_one, w_mid[...], preferred_element_type=F32)
    hidden_two, slope_two = activated(pre_two)
    return own_hidden, hidden_two, slope_one, slope_two


def forward_kernel(mid_rows, place, *refs):
    *sources, w_in, w_mid, own_hidden, hidden_two, slope_one, slope_two = refs
    dom, rep = place[0], place[1]
    values = [feature_rows(source, rep).astype(BF16) for source in sources]
    results = forward(jnp.concatenate(values, axis=1), dom, mid_rows, w_in, w_mid)
    for out, result in zip((own_hidden, hidden_two, slope_one, slope_two), results):
        out[...] = result


def train_kernel(fresh, masks, begun, again, finish, place, *refs):
    if again:
        grads_before, batch_before = refs[:2]
        refs = refs[2:]
    sources = refs[: len(masks)]
    refs = refs[len(masks) :]
    states = refs[:4] if begun else ()
    arranged, slot_rows, w_in, w_mid, w_out, grads, batch, *rest = refs[len(states) :]
    mid_rows = grads.shape[0] - arranged.shape[2]
    dom, rep = place[0], place[1]
    width = batch.shape[1]
    replicas = sources[0].shape[0]
    own_start = (dom * replicas + rep) * width
    values, cots = [], []
    moved = batch_before[...] if again else jnp.zeros(batch.shape, F32)
    for source, mask in zip(sources, masks):
        part = jnp.bitwise_xor(dom, mask)
        value = feature_rows(source, rep)
        spot = lax.broadcasted_iota(jnp.int32, (width, value.shape[1]), 0) + own_start
        chosen = jnp.where(spot.astype(F32) == slot_rows[part], 1.0, 0.0).astype(BF16)
        moved = moved + whole(
            lax.dot_general(pieces(value), chosen, TRAILING, preferred_element_type=F32)
        )
        values.append(value.astype(BF16))
        cots.append(arranged[part])
    batch[...] = moved
    inputs = jnp.concatenate(values, axis=1)
    cot = jnp.concatenate(cots, axis=0)
    done = inputs.shape[1] - fresh
    results = forward(inputs[:, done:], dom, mid_rows, w_in, w_mid)
    if begun:
        results = [
            jnp.concatenate([state[...], result], axis=0) for state, result in zip(states, results)
        ]
    own_hidden, hidden_two, slope_one, slope_two = results
    term = lax.dot_general(cot, hidden_two, LEADING, preferred_element_type=F32)
    grads[mid_rows:, :] = grads_before[mid_rows:, :] + term if again else term
    back_two = jnp.dot(cot, w_out[...], preferred_element_type=F32)
    delta_two = (back_two * slope_two).astype(BF16)
    term = lax.dot_general(own_hidden, delta_two, LEADING, preferred_element_type=F32)
    grads[:mid_rows, :] = grads_before[:mid_rows, :] + term if again else term
    if finish:
        rest[0][...] = input_gradient(inputs, delta_two, slope_one, w_mid)
    else:
        for out, value in zip(rest, (inputs, delta_two, slope_one)):
            out[...] = value


def input_gradient(inputs, delta_two, slope_one, w_mid):
    back_one = lax.dot_general(delta_two, w_mid[...], TRAILING, preferred_element_type=F32)
    delta_one = (back_one * slope_one).astype(BF16)
    return jnp.dot(inputs, delta_one, preferred_element_type=F32)


def last_kernel(before, inputs, delta_two, slope_one, w_mid, grad_in):
    grad_in[...] = before[...] + input_gradient(
        inputs[...], delta_two[...], slope_one[...], w_mid
    )


def add_kernel(split, mine, theirs, *outs):
    start = 0
    for out in outs:
        cut = slice(start, start + out.shape[0]) if split else slice(None)
        out[...] = mine[cut, :] + theirs[cut, :]
        start += out.shape[0]


def call(kernel, outs, scalars, arrays, scratch=(), micros=1.5, space=pltpu.VMEM, mib=16):
    cost = pl.CostEstimate(
        flops=int(micros * 1e9), bytes_accessed=int(micros * 3.6e6), transcendentals=0
    )
    return pl.pallas_call(
        kernel,
        out_shape=outs,
        in_specs=[SMEM] * len(scalars) + [pl.BlockSpec(memory_space=space)] * len(arrays),
        out_specs=jax.tree.map(lambda _: VMEM, outs),
        scratch_shapes=list(scratch),
        compiler_params=pltpu.CompilerParams(vmem_limit_bytes=mib * 2**20),
        cost_estimate=cost,
    )(*scalars, *arrays)


def exchanged(value, mask, devices):
    return lax.ppermute(value, AXES, [(i, i ^ mask) for i in range(devices)])


def gathered_plan(
    features, tiles, tile_row, tile_col, tile_count, dest_slot, w_in, w_mid, w_out, cotangent
):
    owners, replicas = lax.axis_size("dom"), lax.axis_size("rep")
    devices = owners * replicas
    place = jnp.stack([lax.axis_index("dom"), lax.axis_index("rep")]).astype(jnp.int32)
    scalars = [place, tile_count, tile_row, tile_col]
    feature_count, node_count = features.shape
    size = tiles.shape[1]
    classes, width = cotangent.shape
    hidden = w_in.shape[1]
    segment = node_count // devices
    half = node_count // 2
    count = node_count // size
    send = functools.partial(exchanged, devices=devices)
    far_pairs = [
        (d * replicas + r, ((d + 1 if d % 2 else d - 1) % owners) * replicas + r)
        for d in range(owners)
        for r in range(replicas)
    ]

    def far(value):
        return lax.ppermute(value, AXES, far_pairs)

    rows = half // width
    padded = classes + rows + (-(classes + rows)) % 8
    near_one, far_one = send(features, replicas), far(features)
    packed, rank_row = call(
        functools.partial(prepare_kernel, segment, width),
        (
            jax.ShapeDtypeStruct((padded, width), F32),
            jax.ShapeDtypeStruct((1, node_count), jnp.int32),
        ),
        [place],
        [dest_slot.reshape(1, -1), cotangent],
        [
            pltpu.VMEM((1, node_count), jnp.int32),
            pltpu.VMEM((classes, width), BF16),
            pltpu.SemaphoreType.DMA((2,)),
        ],
        space=pltpu.HBM,
    )
    field = pltpu.VMEM((3 * count, 3 * feature_count, size), BF16)
    first = call(
        functools.partial(first_kernel, owners),
        jax.ShapeDtypeStruct(features.shape, F32),
        scalars,
        [features, near_one, far_one, tiles],
        [field],
    )
    line = [packed] + [send(packed, m) for m in (8, 16, 24)]
    column = jnp.stack(line)
    near_two, far_two = send(first, replicas), far(first)
    across_x, across_y = send(column, 4), send(column, 2)
    corner_one, corner_two = send(across_y[0:2], 4), send(across_x[2:4], 2)
    mine, other = call(
        functools.partial(second_kernel, owners),
        tuple(jax.ShapeDtypeStruct((feature_count, half), F32) for _ in range(2)),
        scalars,
        [first, near_two, far_two, tiles, features, rank_row],
        [field],
    )
    own = jnp.stack([mine, send(other, 1), send(mine, 2), send(other, 3)])
    facing = send(own, 4)
    ring = [send(own, m) for m in (8, 16, 24)]
    mid_rows = hidden // owners
    begun = call(
        functools.partial(forward_kernel, mid_rows),
        (
            jax.ShapeDtypeStruct((2 * half, mid_rows), BF16),
            jax.ShapeDtypeStruct((2 * half, hidden), BF16),
            jax.ShapeDtypeStruct((2 * half, hidden), F32),
            jax.ShapeDtypeStruct((2 * half, hidden), F32),
        ),
        [place],
        [own, facing, w_in, w_mid],
        micros=2.5,
        mib=16,
    )
    orders = ((0, 4, 8, 12), (2, 6, 10, 14), (1, 5, 9, 13), (3, 7), (11, 15))
    arranged, slot_rows = call(
        functools.partial(cotangent_kernel, orders, classes, segment),
        (
            jax.ShapeDtypeStruct((owners, half, classes), BF16),
            jax.ShapeDtypeStruct((owners, 1, half), F32),
        ),
        [place],
        [column, across_x, across_y, corner_one, corner_two],
        [
            pltpu.VMEM((devices // 2, classes, width), BF16),
            pltpu.VMEM((devices // 2, rows, width), F32),
        ],
    )
    *ring, gate, slot_rows = lax.optimization_barrier((*ring, begun[0], slot_rows))
    begun = (gate, *begun[1:])
    last = send(jnp.stack(ring), 4)

    feats = feature_count * replicas
    mid_shape = jax.ShapeDtypeStruct((mid_rows, hidden), F32)
    out_shape = jax.ShapeDtypeStruct((classes, hidden), F32)
    grads_shape = jax.ShapeDtypeStruct((mid_rows + classes, hidden), F32)
    in_shape = jax.ShapeDtypeStruct((feats, hidden), F32)
    batch_shape = jax.ShapeDtypeStruct((feats, width), F32)

    def train(before, sources, masks, states, finish, mib):
        fresh = half * (len(masks) - 2 * bool(states))
        rows = half * len(masks)
        rest = (
            (in_shape,)
            if finish
            else (
                jax.ShapeDtypeStruct((feats, rows), BF16),
                jax.ShapeDtypeStruct((rows, hidden), BF16),
                jax.ShapeDtypeStruct((rows, hidden), F32),
            )
        )
        return call(
            functools.partial(train_kernel, fresh, masks, bool(states), bool(before), finish),
            (grads_shape, batch_shape, *rest),
            [place],
            [*before, *sources, *states, arranged, slot_rows, w_in, w_mid, w_out],
            micros=2.5 * len(masks),
            mib=mib,
        )

    grads_before, batch_before, in_before = train((), [own, facing, *ring], (0, 1, 2, 4, 6), begun, True, 32)
    grads, batch_features, *rest = train(
        (grads_before, batch_before), [last[0], last[1], last[2]], (3, 5, 7), (), False, 20
    )
    theirs = send(grads, 1)
    grad_in = call(last_kernel, in_shape, [], [in_before, *rest, w_mid], micros=2.5, mib=12)
    their_in = send(grad_in, 1)
    grad_mid, grad_out = call(
        functools.partial(add_kernel, True), (mid_shape, out_shape), [], [grads, theirs]
    )
    their_in, grad_mid = lax.optimization_barrier((their_in, grad_mid))
    grad_in = call(functools.partial(add_kernel, False), (in_shape,), [], [grad_in, their_in])[0]
    return batch_features, grad_in, grad_mid, grad_out


def extended_2(cells, sides, width):
    for axis, dim in sides:
        count = lax.axis_size(axis)
        head = lax.slice_in_dim(cells, 0, width, axis=dim)
        tail = lax.slice_in_dim(cells, cells.shape[dim] - width, cells.shape[dim], axis=dim)
        cells = jnp.concatenate(
            [
                lax.ppermute(tail, axis, [(i, (i + 1) % count) for i in range(count)]),
                cells,
                lax.ppermute(head, axis, [((i + 1) % count, i) for i in range(count)]),
            ],
            axis=dim,
        )
    return cells


def silu_slope(pre):
    sigma = jax.nn.sigmoid(pre)
    return sigma * (1.0 + pre * (1.0 - sigma))


def neighbour_blocks(local, margin, tile_size):
    extended = extended_2(local, (("dom", 1),), margin * tile_size)
    return extended


def apply_operator(local, tiles_across, assignment_map, relative, margin):
    feature_count, node_count = local.shape
    tile_size = tiles_across.shape[1]
    extended = neighbour_blocks(local, margin, tile_size)
    blocks = extended.reshape(feature_count, -1, tile_size)
    input_values = jnp.take(blocks, relative, axis=1)
    block_products = jnp.einsum(
        "lkz,glz->glk", tiles_across, input_values, precision=lax.Precision.HIGHEST
    )
    final_result = jnp.einsum(
        "wy,kya->kwa", assignment_map, block_products, precision=lax.Precision.HIGHEST
    )
    return final_result.reshape(feature_count, node_count)


def split_plan(
    features, tiles, tile_row, tile_col, tile_count, dest_slot, w_in, w_mid, w_out, cotangent
):
    node_partition = lax.axis_index("dom")
    owners = lax.axis_size("dom")
    replicas = lax.axis_size("rep")
    feature_count, node_count = features.shape
    capacity = tiles.shape[0]
    tile_size = tiles.shape[1]
    block_count = node_count // tile_size
    total_blocks = block_count * owners
    relative = jnp.mod(tile_col - node_partition * block_count + block_count, total_blocks)
    live_mask = (jnp.arange(capacity, dtype=jnp.int32) < tile_count[0]).astype(jnp.float32)
    assignment_map = (
        tile_row[None, :] == jnp.arange(block_count, dtype=jnp.int32)[:, None]
    ).astype(jnp.float32) * live_mask[None, :]
    tiles_across = tiles.astype(jnp.float32)
    first = apply_operator(features, tiles_across, assignment_map, relative, block_count)
    second = (
        2.0 * apply_operator(first, tiles_across, assignment_map, relative, block_count) - features
    )
    diffused = series_zero * features + series_one * first + series_two * second
    segment = node_count // (owners * replicas)
    batch_rows = node_count // replicas
    sort_order = jnp.argsort(dest_slot)
    sorted_slots = jnp.take(dest_slot, sort_order)
    moved_rows = jnp.take(diffused, sort_order, axis=1).reshape(
        feature_count, owners, replicas, segment
    )
    moved_slots = sorted_slots.astype(jnp.float32).reshape(1, owners, replicas, segment)
    arrived, arrived_slots = (
        lax.all_to_all(
            lax.all_to_all(moved_rows, "dom", split_axis=1, concat_axis=1, tiled=True),
            "rep",
            split_axis=2,
            concat_axis=0,
            tiled=True,
        ),
        lax.all_to_all(
            lax.all_to_all(moved_slots, "dom", split_axis=1, concat_axis=1, tiled=True),
            "rep",
            split_axis=2,
            concat_axis=0,
            tiled=True,
        ),
    )
    owner_index = node_partition * replicas + lax.axis_index("rep")
    local_slots = arrived_slots[0].reshape(-1).astype(jnp.int32) - owner_index * batch_rows
    gathered = arrived.reshape(feature_count * replicas, -1)
    batch_features = jnp.zeros(gathered.shape, jnp.float32).at[:, local_slots].set(gathered)
    inputs_bf = batch_features.astype(jnp.bfloat16)
    pre_one = lax.dot_general(inputs_bf, w_in, LEADING, preferred_element_type=jnp.float32)
    hidden_one = jax.nn.silu(pre_one).astype(jnp.bfloat16)
    pre_two = jnp.dot(hidden_one, w_mid, preferred_element_type=jnp.float32)
    hidden_two = jax.nn.silu(pre_two).astype(jnp.bfloat16)
    grad_out = jnp.dot(cotangent, hidden_two, preferred_element_type=jnp.float32)
    back_two = lax.dot_general(cotangent, w_out, LEADING, preferred_element_type=jnp.float32)
    delta_two = (back_two * silu_slope(pre_two)).astype(jnp.bfloat16)
    back_one = lax.dot_general(delta_two, w_mid, TRAILING, preferred_element_type=jnp.float32)
    delta_one = (back_one * silu_slope(pre_one)).astype(jnp.bfloat16)
    grad_in = jnp.dot(inputs_bf, delta_one, preferred_element_type=jnp.float32)
    mid_shard = lax.psum_scatter(
        lax.dot_general(hidden_one, delta_two, LEADING, preferred_element_type=jnp.float32),
        "dom",
        scatter_dimension=0,
        tiled=True,
    )
    grad_mid = lax.psum(mid_shard, "rep")
    grad_in, grad_out = lax.psum((grad_in, grad_out), ("dom", "rep"))
    return (batch_features, grad_in, grad_mid, grad_out)


def solution(mesh):
    compact = mesh.shape["dom"] == 8 and mesh.shape["rep"] == 4
    shards = gathered_plan if compact else split_plan
    in_specs = (
        P("rep", "dom"),
        P("dom", None, None),
        P("dom"),
        P("dom"),
        P("dom"),
        P("dom"),
        P(),
        P(),
        P(),
        P(None, ("dom", "rep")),
    )
    out_specs = (P(None, ("dom", "rep")), P(), P("dom", None), P())
    return jax.shard_map(shards, mesh=mesh, in_specs=in_specs, out_specs=out_specs, check_vma=False)
```

```python
import functools

import jax
import jax.numpy as jnp
from jax import lax
from jax.experimental import pallas as pl
from jax.experimental.pallas import tpu as pltpu
from jax.sharding import PartitionSpec as P

series_zero = 0.3085083
series_one = -0.4305395
series_two = 0.1864784
LEADING = (((0,), (0,)), ((), ()))
TRAILING = (((1,), (1,)), ((), ()))
AXES = ("dom", "rep")
F32 = jnp.float32
BF16 = jnp.bfloat16
VMEM = pl.BlockSpec(memory_space=pltpu.VMEM)
SMEM = pl.BlockSpec(memory_space=pltpu.SMEM)


def pieces(value):
    high = value.astype(BF16)
    rest = value - high.astype(F32)
    middle = rest.astype(BF16)
    low = (rest - middle.astype(F32)).astype(BF16)
    return jnp.concatenate([high, middle, low], axis=0)


def whole(parts):
    rows = parts.shape[0] // 3
    return parts[:rows] + parts[rows : 2 * rows] + parts[2 * rows :]


def prepare_kernel(segment, block, place, slots_hbm, cot_hbm, packed, rank_row, slots, cot, sems):
    fetch_slots = pltpu.make_async_copy(slots_hbm, slots, sems.at[0])
    fetch_cot = pltpu.make_async_copy(cot_hbm, cot, sems.at[1])
    fetch_slots.start()
    fetch_cot.start()
    fetch_slots.wait()
    nodes = slots.shape[1]
    half = nodes // 2
    row = slots[...].astype(F32)
    column = jnp.broadcast_to(row, (8, nodes)).T[:, 0:1]
    wide = jnp.broadcast_to(row, (nodes, nodes))
    order = jnp.sum(jnp.where(column < wide, 1.0, 0.0), axis=0, keepdims=True).astype(jnp.int32)
    target = slots[...] // block
    rank = (target % 2) * half + (target // 2) * segment + order - target * segment
    rank_row[...] = rank
    rank_column = jnp.broadcast_to(rank.astype(F32), (8, nodes)).T[:, 0:1]
    lane = lax.broadcasted_iota(jnp.int32, (nodes, nodes), 1).astype(F32)
    ordered = jnp.sum(jnp.where(rank_column == lane, column, 0.0), axis=0, keepdims=True)
    mine = jnp.where(place[1] % 2 == 0, ordered[:, :half], ordered[:, half:])
    classes, width = cot.shape
    fetch_cot.wait()
    packed[0:classes, :] = cot[...].astype(F32)
    extra = packed.shape[0] - classes
    rows = half // width
    for index in range(rows):
        packed[classes + index : classes + index + 1, :] = mine[:, index * width : (index + 1) * width]
    if extra > rows:
        packed[classes + rows :, :] = jnp.zeros((extra - rows, width), F32)


def operate(place, live, row, col, own, near, far, tiles, field, owners):
    capacity, size, _ = tiles.shape
    count = own.shape[1] // size
    dom = place[0]
    odd = dom % 2
    near_base = (1 - odd) * 2 * count
    far_base = odd * 2 * count
    for index in range(count):
        cut = slice(index * size, (index + 1) * size)
        field[count + index] = pieces(own[:, cut])
        field[near_base + index] = pieces(near[:, cut])
        field[far_base + index] = pieces(far[:, cut])
    total = count * owners
    sums = [jnp.zeros((own.shape[0], size), F32) for _ in range(count)]
    for slot in range(capacity):
        relative = lax.rem(col[slot] - dom * count + count + total, total)
        target = jnp.where(slot < live[0], row[slot], -1)
        product = whole(
            lax.dot_general(field[relative], tiles[slot], TRAILING, preferred_element_type=F32)
        )
        for index in range(count):
            sums[index] = sums[index] + jnp.where(target == index, product, 0.0)
    return jnp.concatenate(sums, axis=1)


def first_kernel(owners, place, live, row, col, own, near, far, tiles, first, field):
    first[...] = operate(place, live, row, col, own, near, far, tiles, field, owners)


def second_kernel(
    owners, place, live, row, col, own, near, far, tiles, features, rank_row, mine, other, field
):
    applied = operate(place, live, row, col, own, near, far, tiles, field, owners)
    base = features[...]
    second = 2.0 * applied - base
    diffused = series_zero * base + series_one * own[...] + series_two * second
    nodes = base.shape[1]
    spot = lax.broadcasted_iota(jnp.int32, (nodes, nodes), 0)
    chosen = jnp.where(spot == rank_row[...], 1.0, 0.0).astype(BF16)
    ordered = whole(lax.dot_general(pieces(diffused), chosen, TRAILING, preferred_element_type=F32))
    low, high = ordered[:, : nodes // 2], ordered[:, nodes // 2 :]
    core = place[1] % 2
    mine[...] = jnp.where(core == 0, low, high)
    other[...] = jnp.where(core == 0, high, low)


def cotangent_kernel(orders, classes, segment, place, *refs):
    sources = refs[: len(orders)]
    arranged, slot_rows, held, listed = refs[len(orders) :]
    me = place[0] * 2 + place[1] // 2
    core = place[1] % 2
    blocks = held.shape[0]
    width = held.shape[2]
    parts = arranged.shape[0]
    rows = listed.shape[1]
    for source, order in zip(sources, orders):
        for index, mask in enumerate(order):
            block = jnp.bitwise_xor(me, mask)
            held[block] = source[index, 0:classes, :].astype(BF16)
            listed[block] = source[index, classes : classes + rows, :]
    lists = []
    for part in range(parts):
        listing = listed[2 * part]
        row = jnp.concatenate([listing[i : i + 1] for i in range(rows)], axis=1)
        slot_rows[part] = row
        lists.append(row)
    columns = jnp.concatenate(lists, axis=0).T
    lane = lax.broadcasted_iota(jnp.int32, (segment, width), 1).astype(F32)
    for block in range(blocks):
        start = ((2 * block + core) * width).astype(F32)
        cut = slice(block * segment, (block + 1) * segment)
        chosen = jnp.concatenate(
            [
                jnp.where(columns[cut, part : part + 1] - start == lane, 1.0, 0.0)
                for part in range(parts)
            ],
            axis=0,
        ).astype(BF16)
        moved = lax.dot_general(chosen, held[block], TRAILING, preferred_element_type=F32)
        for part in range(parts):
            arranged[part, cut, :] = moved[part * segment : (part + 1) * segment].astype(BF16)


def activated(pre):
    gate = 0.5 * jnp.tanh(0.5 * pre) + 0.5
    value = pre * gate
    return value.astype(BF16), gate + value * (1.0 - gate)


def feature_rows(source, rep):
    replicas = source.shape[0]
    return jnp.concatenate([source[jnp.bitwise_xor(rep, i)] for i in range(replicas)], axis=0)


def forward(inputs, dom, mid_rows, w_in, w_mid):
    pre_one = lax.dot_general(inputs, w_in[...], LEADING, preferred_element_type=F32)
    hidden_one, slope_one = activated(pre_one)
    own_pre = lax.dot_general(
        inputs,
        w_in[:, pl.ds(pl.multiple_of(dom * mid_rows, mid_rows), mid_rows)],
        LEADING,
        preferred_element_type=F32,
    )
    own_hidden, _ = activated(own_pre)
    pre_two = jnp.dot(hidden_one, w_mid[...], preferred_element_type=F32)
    hidden_two, slope_two = activated(pre_two)
    return own_hidden, hidden_two, slope_one, slope_two


def forward_kernel(mid_rows, place, *refs):
    *sources, w_in, w_mid, own_hidden, hidden_two, slope_one, slope_two = refs
    dom, rep = place[0], place[1]
    values = [feature_rows(source, rep).astype(BF16) for source in sources]
    results = forward(jnp.concatenate(values, axis=1), dom, mid_rows, w_in, w_mid)
    for out, result in zip((own_hidden, hidden_two, slope_one, slope_two), results):
        out[...] = result


def train_kernel(fresh, masks, begun, again, finish, place, *refs):
    if again:
        grads_before, batch_before = refs[:2]
        refs = refs[2:]
    sources = refs[: len(masks)]
    refs = refs[len(masks) :]
    states = refs[:4] if begun else ()
    arranged, slot_rows, w_in, w_mid, w_out, grads, batch, *rest = refs[len(states) :]
    mid_rows = grads.shape[0] - arranged.shape[2]
    dom, rep = place[0], place[1]
    width = batch.shape[1]
    replicas = sources[0].shape[0]
    own_start = (dom * replicas + rep) * width
    values, cots = [], []
    moved = batch_before[...] if again else jnp.zeros(batch.shape, F32)
    for source, mask in zip(sources, masks):
        part = jnp.bitwise_xor(dom, mask)
        value = feature_rows(source, rep)
        spot = lax.broadcasted_iota(jnp.int32, (width, value.shape[1]), 0) + own_start
        chosen = jnp.where(spot.astype(F32) == slot_rows[part], 1.0, 0.0).astype(BF16)
        moved = moved + whole(
            lax.dot_general(pieces(value), chosen, TRAILING, preferred_element_type=F32)
        )
        values.append(value.astype(BF16))
        cots.append(arranged[part])
    batch[...] = moved
    inputs = jnp.concatenate(values, axis=1)
    cot = jnp.concatenate(cots, axis=0)
    done = inputs.shape[1] - fresh
    results = forward(inputs[:, done:], dom, mid_rows, w_in, w_mid)
    if begun:
        results = [
            jnp.concatenate([state[...], result], axis=0) for state, result in zip(states, results)
        ]
    own_hidden, hidden_two, slope_one, slope_two = results
    term = lax.dot_general(cot, hidden_two, LEADING, preferred_element_type=F32)
    grads[mid_rows:, :] = grads_before[mid_rows:, :] + term if again else term
    back_two = jnp.dot(cot, w_out[...], preferred_element_type=F32)
    delta_two = (back_two * slope_two).astype(BF16)
    term = lax.dot_general(own_hidden, delta_two, LEADING, preferred_element_type=F32)
    grads[:mid_rows, :] = grads_before[:mid_rows, :] + term if again else term
    if finish:
        rest[0][...] = input_gradient(inputs, delta_two, slope_one, w_mid)
    else:
        for out, value in zip(rest, (inputs, delta_two, slope_one)):
            out[...] = value


def input_gradient(inputs, delta_two, slope_one, w_mid):
    back_one = lax.dot_general(delta_two, w_mid[...], TRAILING, preferred_element_type=F32)
    delta_one = (back_one * slope_one).astype(BF16)
    return jnp.dot(inputs, delta_one, preferred_element_type=F32)


def last_kernel(before, inputs, delta_two, slope_one, w_mid, grad_in):
    grad_in[...] = before[...] + input_gradient(
        inputs[...], delta_two[...], slope_one[...], w_mid
    )


def add_kernel(split, mine, theirs, *outs):
    start = 0
    for out in outs:
        cut = slice(start, start + out.shape[0]) if split else slice(None)
        out[...] = mine[cut, :] + theirs[cut, :]
        start += out.shape[0]


def call(kernel, outs, scalars, arrays, scratch=(), micros=1.5, space=pltpu.VMEM, mib=16):
    cost = pl.CostEstimate(
        flops=int(micros * 1e9), bytes_accessed=int(micros * 3.6e6), transcendentals=0
    )
    return pl.pallas_call(
        kernel,
        out_shape=outs,
        in_specs=[SMEM] * len(scalars) + [pl.BlockSpec(memory_space=space)] * len(arrays),
        out_specs=jax.tree.map(lambda _: VMEM, outs),
        scratch_shapes=list(scratch),
        compiler_params=pltpu.CompilerParams(vmem_limit_bytes=mib * 2**20),
        cost_estimate=cost,
    )(*scalars, *arrays)


def exchanged(value, mask, devices):
    return lax.ppermute(value, AXES, [(i, i ^ mask) for i in range(devices)])


def gathered_plan(
    features, tiles, tile_row, tile_col, tile_count, dest_slot, w_in, w_mid, w_out, cotangent
):
    owners, replicas = lax.axis_size("dom"), lax.axis_size("rep")
    devices = owners * replicas
    place = jnp.stack([lax.axis_index("dom"), lax.axis_index("rep")]).astype(jnp.int32)
    scalars = [place, tile_count, tile_row, tile_col]
    feature_count, node_count = features.shape
    size = tiles.shape[1]
    classes, width = cotangent.shape
    hidden = w_in.shape[1]
    segment = node_count // devices
    half = node_count // 2
    count = node_count // size
    send = functools.partial(exchanged, devices=devices)
    far_pairs = [
        (d * replicas + r, ((d + 1 if d % 2 else d - 1) % owners) * replicas + r)
        for d in range(owners)
        for r in range(replicas)
    ]

    def far(value):
        return lax.ppermute(value, AXES, far_pairs)

    rows = half // width
    padded = classes + rows + (-(classes + rows)) % 8
    near_one, far_one = send(features, replicas), far(features)
    packed, rank_row = call(
        functools.partial(prepare_kernel, segment, width),
        (
            jax.ShapeDtypeStruct((padded, width), F32),
            jax.ShapeDtypeStruct((1, node_count), jnp.int32),
        ),
        [place],
        [dest_slot.reshape(1, -1), cotangent],
        [
            pltpu.VMEM((1, node_count), jnp.int32),
            pltpu.VMEM((classes, width), BF16),
            pltpu.SemaphoreType.DMA((2,)),
        ],
        space=pltpu.HBM,
    )
    field = pltpu.VMEM((3 * count, 3 * feature_count, size), BF16)
    first = call(
        functools.partial(first_kernel, owners),
        jax.ShapeDtypeStruct(features.shape, F32),
        scalars,
        [features, near_one, far_one, tiles],
        [field],
    )
    line = [packed] + [send(packed, m) for m in (8, 16, 24)]
    column = jnp.stack(line)
    near_two, far_two = send(first, replicas), far(first)
    across_x, across_y = send(column, 4), send(column, 2)
    corner_one, corner_two = send(across_y[0:2], 4), send(across_x[2:4], 2)
    mine, other = call(
        functools.partial(second_kernel, owners),
        tuple(jax.ShapeDtypeStruct((feature_count, half), F32) for _ in range(2)),
        scalars,
        [first, near_two, far_two, tiles, features, rank_row],
        [field],
    )
    own = jnp.stack([mine, send(other, 1), send(mine, 2), send(other, 3)])
    facing = send(own, 4)
    ring = [send(own, m) for m in (24, 16)]
    near_line = send(own, 8)
    mid_rows = hidden // owners
    begun = call(
        functools.partial(forward_kernel, mid_rows),
        (
            jax.ShapeDtypeStruct((3 * half, mid_rows), BF16),
            jax.ShapeDtypeStruct((3 * half, hidden), BF16),
            jax.ShapeDtypeStruct((3 * half, hidden), F32),
            jax.ShapeDtypeStruct((3 * half, hidden), F32),
        ),
        [place],
        [own, facing, near_line, w_in, w_mid],
        micros=3.7,
        mib=20,
    )
    orders = ((0, 4, 8, 12), (2, 6, 10, 14), (1, 5, 9, 13), (3, 7), (11, 15))
    arranged, slot_rows = call(
        functools.partial(cotangent_kernel, orders, classes, segment),
        (
            jax.ShapeDtypeStruct((owners, half, classes), BF16),
            jax.ShapeDtypeStruct((owners, 1, half), F32),
        ),
        [place],
        [column, across_x, across_y, corner_one, corner_two],
        [
            pltpu.VMEM((devices // 2, classes, width), BF16),
            pltpu.VMEM((devices // 2, rows, width), F32),
        ],
    )
    near_ready, *begun = lax.optimization_barrier((near_line, *begun))
    near_across = send(near_ready, 4)
    *ring, gate, slot_rows = lax.optimization_barrier((*ring, begun[0], slot_rows))
    begun = (gate, *begun[1:])
    last = send(jnp.stack(ring), 4)

    feats = feature_count * replicas
    mid_shape = jax.ShapeDtypeStruct((mid_rows, hidden), F32)
    out_shape = jax.ShapeDtypeStruct((classes, hidden), F32)
    grads_shape = jax.ShapeDtypeStruct((mid_rows + classes, hidden), F32)
    in_shape = jax.ShapeDtypeStruct((feats, hidden), F32)
    batch_shape = jax.ShapeDtypeStruct((feats, width), F32)

    def train(before, sources, masks, states, finish, mib):
        fresh = half * (len(masks) - 3 * bool(states))
        rows = half * len(masks)
        rest = (
            (in_shape,)
            if finish
            else (
                jax.ShapeDtypeStruct((feats, rows), BF16),
                jax.ShapeDtypeStruct((rows, hidden), BF16),
                jax.ShapeDtypeStruct((rows, hidden), F32),
            )
        )
        return call(
            functools.partial(train_kernel, fresh, masks, bool(states), bool(before), finish),
            (grads_shape, batch_shape, *rest),
            [place],
            [*before, *sources, *states, arranged, slot_rows, w_in, w_mid, w_out],
            micros=2.5 * len(masks),
            mib=mib,
        )

    grads_before, batch_before, in_before = train(
        (), [own, facing, near_line, *ring], (0, 1, 2, 6, 4), begun, True, 32
    )
    grads, batch_features, *rest = train(
        (grads_before, batch_before), [near_across, last[0], last[1]], (3, 7, 5), (), False, 20
    )
    theirs = send(grads, 1)
    grad_in = call(last_kernel, in_shape, [], [in_before, *rest, w_mid], micros=2.5, mib=12)
    their_in = send(grad_in, 1)
    grad_mid, grad_out = call(
        functools.partial(add_kernel, True), (mid_shape, out_shape), [], [grads, theirs]
    )
    their_in, grad_mid = lax.optimization_barrier((their_in, grad_mid))
    grad_in = call(functools.partial(add_kernel, False), (in_shape,), [], [grad_in, their_in])[0]
    return batch_features, grad_in, grad_mid, grad_out


def extended_2(cells, sides, width):
    for axis, dim in sides:
        count = lax.axis_size(axis)
        head = lax.slice_in_dim(cells, 0, width, axis=dim)
        tail = lax.slice_in_dim(cells, cells.shape[dim] - width, cells.shape[dim], axis=dim)
        cells = jnp.concatenate(
            [
                lax.ppermute(tail, axis, [(i, (i + 1) % count) for i in range(count)]),
                cells,
                lax.ppermute(head, axis, [((i + 1) % count, i) for i in range(count)]),
            ],
            axis=dim,
        )
    return cells


def silu_slope(pre):
    sigma = jax.nn.sigmoid(pre)
    return sigma * (1.0 + pre * (1.0 - sigma))


def neighbour_blocks(local, margin, tile_size):
    extended = extended_2(local, (("dom", 1),), margin * tile_size)
    return extended


def apply_operator(local, tiles_across, assignment_map, relative, margin):
    feature_count, node_count = local.shape
    tile_size = tiles_across.shape[1]
    extended = neighbour_blocks(local, margin, tile_size)
    blocks = extended.reshape(feature_count, -1, tile_size)
    input_values = jnp.take(blocks, relative, axis=1)
    block_products = jnp.einsum(
        "lkz,glz->glk", tiles_across, input_values, precision=lax.Precision.HIGHEST
    )
    final_result = jnp.einsum(
        "wy,kya->kwa", assignment_map, block_products, precision=lax.Precision.HIGHEST
    )
    return final_result.reshape(feature_count, node_count)


def split_plan(
    features, tiles, tile_row, tile_col, tile_count, dest_slot, w_in, w_mid, w_out, cotangent
):
    node_partition = lax.axis_index("dom")
    owners = lax.axis_size("dom")
    replicas = lax.axis_size("rep")
    feature_count, node_count = features.shape
    capacity = tiles.shape[0]
    tile_size = tiles.shape[1]
    block_count = node_count // tile_size
    total_blocks = block_count * owners
    relative = jnp.mod(tile_col - node_partition * block_count + block_count, total_blocks)
    live_mask = (jnp.arange(capacity, dtype=jnp.int32) < tile_count[0]).astype(jnp.float32)
    assignment_map = (
        tile_row[None, :] == jnp.arange(block_count, dtype=jnp.int32)[:, None]
    ).astype(jnp.float32) * live_mask[None, :]
    tiles_across = tiles.astype(jnp.float32)
    first = apply_operator(features, tiles_across, assignment_map, relative, block_count)
    second = (
        2.0 * apply_operator(first, tiles_across, assignment_map, relative, block_count) - features
    )
    diffused = series_zero * features + series_one * first + series_two * second
    segment = node_count // (owners * replicas)
    batch_rows = node_count // replicas
    sort_order = jnp.argsort(dest_slot)
    sorted_slots = jnp.take(dest_slot, sort_order)
    moved_rows = jnp.take(diffused, sort_order, axis=1).reshape(
        feature_count, owners, replicas, segment
    )
    moved_slots = sorted_slots.astype(jnp.float32).reshape(1, owners, replicas, segment)
    arrived, arrived_slots = (
        lax.all_to_all(
            lax.all_to_all(moved_rows, "dom", split_axis=1, concat_axis=1, tiled=True),
            "rep",
            split_axis=2,
            concat_axis=0,
            tiled=True,
        ),
        lax.all_to_all(
            lax.all_to_all(moved_slots, "dom", split_axis=1, concat_axis=1, tiled=True),
            "rep",
            split_axis=2,
            concat_axis=0,
            tiled=True,
        ),
    )
    owner_index = node_partition * replicas + lax.axis_index("rep")
    local_slots = arrived_slots[0].reshape(-1).astype(jnp.int32) - owner_index * batch_rows
    gathered = arrived.reshape(feature_count * replicas, -1)
    batch_features = jnp.zeros(gathered.shape, jnp.float32).at[:, local_slots].set(gathered)
    inputs_bf = batch_features.astype(jnp.bfloat16)
    pre_one = lax.dot_general(inputs_bf, w_in, LEADING, preferred_element_type=jnp.float32)
    hidden_one = jax.nn.silu(pre_one).astype(jnp.bfloat16)
    pre_two = jnp.dot(hidden_one, w_mid, preferred_element_type=jnp.float32)
    hidden_two = jax.nn.silu(pre_two).astype(jnp.bfloat16)
    grad_out = jnp.dot(cotangent, hidden_two, preferred_element_type=jnp.float32)
    back_two = lax.dot_general(cotangent, w_out, LEADING, preferred_element_type=jnp.float32)
    delta_two = (back_two * silu_slope(pre_two)).astype(jnp.bfloat16)
    back_one = lax.dot_general(delta_two, w_mid, TRAILING, preferred_element_type=jnp.float32)
    delta_one = (back_one * silu_slope(pre_one)).astype(jnp.bfloat16)
    grad_in = jnp.dot(inputs_bf, delta_one, preferred_element_type=jnp.float32)
    mid_shard = lax.psum_scatter(
        lax.dot_general(hidden_one, delta_two, LEADING, preferred_element_type=jnp.float32),
        "dom",
        scatter_dimension=0,
        tiled=True,
    )
    grad_mid = lax.psum(mid_shard, "rep")
    grad_in, grad_out = lax.psum((grad_in, grad_out), ("dom", "rep"))
    return (batch_features, grad_in, grad_mid, grad_out)


def solution(mesh):
    compact = mesh.shape["dom"] == 8 and mesh.shape["rep"] == 4
    shards = gathered_plan if compact else split_plan
    in_specs = (
        P("rep", "dom"),
        P("dom", None, None),
        P("dom"),
        P("dom"),
        P("dom"),
        P("dom"),
        P(),
        P(),
        P(),
        P(None, ("dom", "rep")),
    )
    out_specs = (P(None, ("dom", "rep")), P(), P("dom", None), P())
    return jax.shard_map(shards, mesh=mesh, in_specs=in_specs, out_specs=out_specs, check_vma=False)
```

```python
import functools

import jax
import jax.numpy as jnp
from jax import lax
from jax.experimental import pallas as pl
from jax.experimental.pallas import tpu as pltpu
from jax.sharding import PartitionSpec as P

series_zero = 0.3085083
series_one = -0.4305395
series_two = 0.1864784
LEADING = (((0,), (0,)), ((), ()))
TRAILING = (((1,), (1,)), ((), ()))
AXES = ("dom", "rep")
F32 = jnp.float32
BF16 = jnp.bfloat16
VMEM = pl.BlockSpec(memory_space=pltpu.VMEM)
SMEM = pl.BlockSpec(memory_space=pltpu.SMEM)


def pieces(value):
    high = value.astype(BF16)
    rest = value - high.astype(F32)
    middle = rest.astype(BF16)
    low = (rest - middle.astype(F32)).astype(BF16)
    return jnp.concatenate([high, middle, low], axis=0)


def whole(parts):
    rows = parts.shape[0] // 3
    return parts[:rows] + parts[rows : 2 * rows] + parts[2 * rows :]


def open_kernel(place, out):
    out[...] = jnp.full(out.shape, place[0], F32)


def prepare_kernel(segment, block, place, slots_hbm, cot_hbm, opened, packed, rank_row, slots, cot, sems):
    fetch_slots = pltpu.make_async_copy(slots_hbm, slots, sems.at[0])
    fetch_cot = pltpu.make_async_copy(cot_hbm, cot, sems.at[1])
    fetch_slots.start()
    fetch_cot.start()
    fetch_slots.wait()
    nodes = slots.shape[1]
    half = nodes // 2
    row = slots[...].astype(F32)
    column = jnp.broadcast_to(row, (8, nodes)).T[:, 0:1]
    wide = jnp.broadcast_to(row, (nodes, nodes))
    order = jnp.sum(jnp.where(column < wide, 1.0, 0.0), axis=0, keepdims=True).astype(jnp.int32)
    target = slots[...] // block
    rank = (target % 2) * half + (target // 2) * segment + order - target * segment
    rank_row[...] = rank
    rank_column = jnp.broadcast_to(rank.astype(F32), (8, nodes)).T[:, 0:1]
    lane = lax.broadcasted_iota(jnp.int32, (nodes, nodes), 1).astype(F32)
    ordered = jnp.sum(jnp.where(rank_column == lane, column, 0.0), axis=0, keepdims=True)
    mine = jnp.where(place[1] % 2 == 0, ordered[:, :half], ordered[:, half:])
    classes, width = cot.shape
    fetch_cot.wait()
    packed[0:classes, :] = cot[...].astype(F32)
    extra = packed.shape[0] - classes
    rows = half // width
    for index in range(rows):
        packed[classes + index : classes + index + 1, :] = mine[:, index * width : (index + 1) * width]
    if extra > rows:
        packed[classes + rows :, :] = jnp.zeros((extra - rows, width), F32)


def operate(place, live, row, col, own, near, far, tiles, field, owners):
    capacity, size, _ = tiles.shape
    count = own.shape[1] // size
    dom = place[0]
    odd = dom % 2
    near_base = (1 - odd) * 2 * count
    far_base = odd * 2 * count
    for index in range(count):
        cut = slice(index * size, (index + 1) * size)
        field[count + index] = pieces(own[:, cut])
        field[near_base + index] = pieces(near[:, cut])
        field[far_base + index] = pieces(far[:, cut])
    total = count * owners
    sums = [jnp.zeros((own.shape[0], size), F32) for _ in range(count)]
    for slot in range(capacity):
        relative = lax.rem(col[slot] - dom * count + count + total, total)
        target = jnp.where(slot < live[0], row[slot], -1)
        product = whole(
            lax.dot_general(field[relative], tiles[slot], TRAILING, preferred_element_type=F32)
        )
        for index in range(count):
            sums[index] = sums[index] + jnp.where(target == index, product, 0.0)
    return jnp.concatenate(sums, axis=1)


def first_kernel(owners, place, live, row, col, own, near, far, tiles, first, field):
    first[...] = operate(place, live, row, col, own, near, far, tiles, field, owners)


def second_kernel(
    owners, place, live, row, col, own, near, far, tiles, features, rank_row, mine, other, field
):
    applied = operate(place, live, row, col, own, near, far, tiles, field, owners)
    base = features[...]
    second = 2.0 * applied - base
    diffused = series_zero * base + series_one * own[...] + series_two * second
    nodes = base.shape[1]
    spot = lax.broadcasted_iota(jnp.int32, (nodes, nodes), 0)
    chosen = jnp.where(spot == rank_row[...], 1.0, 0.0).astype(BF16)
    ordered = whole(lax.dot_general(pieces(diffused), chosen, TRAILING, preferred_element_type=F32))
    low, high = ordered[:, : nodes // 2], ordered[:, nodes // 2 :]
    core = place[1] % 2
    mine[...] = jnp.where(core == 0, low, high)
    other[...] = jnp.where(core == 0, high, low)


def cotangent_kernel(orders, classes, segment, place, *refs):
    sources = refs[: len(orders)]
    arranged, slot_rows, held, listed = refs[len(orders) :]
    me = place[0] * 2 + place[1] // 2
    core = place[1] % 2
    blocks = held.shape[0]
    width = held.shape[2]
    parts = arranged.shape[0]
    rows = listed.shape[1]
    for source, order in zip(sources, orders):
        for index, mask in enumerate(order):
            block = jnp.bitwise_xor(me, mask)
            held[block] = source[index, 0:classes, :].astype(BF16)
            listed[block] = source[index, classes : classes + rows, :]
    lists = []
    for part in range(parts):
        listing = listed[2 * part]
        row = jnp.concatenate([listing[i : i + 1] for i in range(rows)], axis=1)
        slot_rows[part] = row
        lists.append(row)
    columns = jnp.concatenate(lists, axis=0).T
    lane = lax.broadcasted_iota(jnp.int32, (segment, width), 1).astype(F32)
    for block in range(blocks):
        start = ((2 * block + core) * width).astype(F32)
        cut = slice(block * segment, (block + 1) * segment)
        chosen = jnp.concatenate(
            [
                jnp.where(columns[cut, part : part + 1] - start == lane, 1.0, 0.0)
                for part in range(parts)
            ],
            axis=0,
        ).astype(BF16)
        moved = lax.dot_general(chosen, held[block], TRAILING, preferred_element_type=F32)
        for part in range(parts):
            arranged[part, cut, :] = moved[part * segment : (part + 1) * segment].astype(BF16)


def activated(pre):
    gate = 0.5 * jnp.tanh(0.5 * pre) + 0.5
    value = pre * gate
    return value.astype(BF16), gate + value * (1.0 - gate)


def feature_rows(source, rep):
    replicas = source.shape[0]
    return jnp.concatenate([source[jnp.bitwise_xor(rep, i)] for i in range(replicas)], axis=0)


def forward(inputs, dom, mid_rows, w_in, w_mid):
    pre_one = lax.dot_general(inputs, w_in[...], LEADING, preferred_element_type=F32)
    hidden_one, slope_one = activated(pre_one)
    own_pre = lax.dot_general(
        inputs,
        w_in[:, pl.ds(pl.multiple_of(dom * mid_rows, mid_rows), mid_rows)],
        LEADING,
        preferred_element_type=F32,
    )
    own_hidden, _ = activated(own_pre)
    pre_two = jnp.dot(hidden_one, w_mid[...], preferred_element_type=F32)
    hidden_two, slope_two = activated(pre_two)
    return own_hidden, hidden_two, slope_one, slope_two


def forward_kernel(mid_rows, place, *refs):
    *sources, w_in, w_mid, own_hidden, hidden_two, slope_one, slope_two = refs
    dom, rep = place[0], place[1]
    values = [feature_rows(source, rep).astype(BF16) for source in sources]
    results = forward(jnp.concatenate(values, axis=1), dom, mid_rows, w_in, w_mid)
    for out, result in zip((own_hidden, hidden_two, slope_one, slope_two), results):
        out[...] = result


def train_kernel(fresh, masks, begun, again, finish, place, *refs):
    if again:
        grads_before, batch_before = refs[:2]
        refs = refs[2:]
    sources = refs[: len(masks)]
    refs = refs[len(masks) :]
    states = refs[:4] if begun else ()
    arranged, slot_rows, w_in, w_mid, w_out, grads, batch, *rest = refs[len(states) :]
    mid_rows = grads.shape[0] - arranged.shape[2]
    dom, rep = place[0], place[1]
    width = batch.shape[1]
    replicas = sources[0].shape[0]
    own_start = (dom * replicas + rep) * width
    values, cots = [], []
    moved = batch_before[...] if again else jnp.zeros(batch.shape, F32)
    for source, mask in zip(sources, masks):
        part = jnp.bitwise_xor(dom, mask)
        value = feature_rows(source, rep)
        spot = lax.broadcasted_iota(jnp.int32, (width, value.shape[1]), 0) + own_start
        chosen = jnp.where(spot.astype(F32) == slot_rows[part], 1.0, 0.0).astype(BF16)
        moved = moved + whole(
            lax.dot_general(pieces(value), chosen, TRAILING, preferred_element_type=F32)
        )
        values.append(value.astype(BF16))
        cots.append(arranged[part])
    batch[...] = moved
    inputs = jnp.concatenate(values, axis=1)
    cot = jnp.concatenate(cots, axis=0)
    done = inputs.shape[1] - fresh
    results = forward(inputs[:, done:], dom, mid_rows, w_in, w_mid)
    if begun:
        results = [
            jnp.concatenate([state[...], result], axis=0) for state, result in zip(states, results)
        ]
    own_hidden, hidden_two, slope_one, slope_two = results
    term = lax.dot_general(cot, hidden_two, LEADING, preferred_element_type=F32)
    grads[mid_rows:, :] = grads_before[mid_rows:, :] + term if again else term
    back_two = jnp.dot(cot, w_out[...], preferred_element_type=F32)
    delta_two = (back_two * slope_two).astype(BF16)
    term = lax.dot_general(own_hidden, delta_two, LEADING, preferred_element_type=F32)
    grads[:mid_rows, :] = grads_before[:mid_rows, :] + term if again else term
    if finish:
        rest[0][...] = input_gradient(inputs, delta_two, slope_one, w_mid)
    else:
        for out, value in zip(rest, (inputs, delta_two, slope_one)):
            out[...] = value


def input_gradient(inputs, delta_two, slope_one, w_mid):
    back_one = lax.dot_general(delta_two, w_mid[...], TRAILING, preferred_element_type=F32)
    delta_one = (back_one * slope_one).astype(BF16)
    return jnp.dot(inputs, delta_one, preferred_element_type=F32)


def last_kernel(before, inputs, delta_two, slope_one, w_mid, grad_in):
    grad_in[...] = before[...] + input_gradient(
        inputs[...], delta_two[...], slope_one[...], w_mid
    )


def add_kernel(split, mine, theirs, *outs):
    start = 0
    for out in outs:
        cut = slice(start, start + out.shape[0]) if split else slice(None)
        out[...] = mine[cut, :] + theirs[cut, :]
        start += out.shape[0]


def call(kernel, outs, scalars, arrays, scratch=(), micros=1.5, space=pltpu.VMEM, mib=16):
    cost = pl.CostEstimate(
        flops=int(micros * 1e9), bytes_accessed=int(micros * 3.6e6), transcendentals=0
    )
    return pl.pallas_call(
        kernel,
        out_shape=outs,
        in_specs=[SMEM] * len(scalars) + [pl.BlockSpec(memory_space=space)] * len(arrays),
        out_specs=jax.tree.map(lambda _: VMEM, outs),
        scratch_shapes=list(scratch),
        compiler_params=pltpu.CompilerParams(vmem_limit_bytes=mib * 2**20),
        cost_estimate=cost,
    )(*scalars, *arrays)


def exchanged(value, mask, devices):
    return lax.ppermute(value, AXES, [(i, i ^ mask) for i in range(devices)])


def gathered_plan(
    features, tiles, tile_row, tile_col, tile_count, dest_slot, w_in, w_mid, w_out, cotangent
):
    owners, replicas = lax.axis_size("dom"), lax.axis_size("rep")
    devices = owners * replicas
    place = jnp.stack([lax.axis_index("dom"), lax.axis_index("rep")]).astype(jnp.int32)
    scalars = [place, tile_count, tile_row, tile_col]
    feature_count, node_count = features.shape
    size = tiles.shape[1]
    classes, width = cotangent.shape
    hidden = w_in.shape[1]
    segment = node_count // devices
    half = node_count // 2
    count = node_count // size
    send = functools.partial(exchanged, devices=devices)
    far_pairs = [
        (d * replicas + r, ((d + 1 if d % 2 else d - 1) % owners) * replicas + r)
        for d in range(owners)
        for r in range(replicas)
    ]

    def far(value):
        return lax.ppermute(value, AXES, far_pairs)

    rows = half // width
    padded = classes + rows + (-(classes + rows)) % 8
    opened = call(open_kernel, jax.ShapeDtypeStruct((8, 128), F32), [place], [], micros=4.0)
    opened, ready = lax.optimization_barrier((opened, features))
    near_one, far_one = send(ready, replicas), far(ready)
    packed, rank_row = call(
        functools.partial(prepare_kernel, segment, width),
        (
            jax.ShapeDtypeStruct((padded, width), F32),
            jax.ShapeDtypeStruct((1, node_count), jnp.int32),
        ),
        [place],
        [dest_slot.reshape(1, -1), cotangent, opened],
        [
            pltpu.VMEM((1, node_count), jnp.int32),
            pltpu.VMEM((classes, width), BF16),
            pltpu.SemaphoreType.DMA((2,)),
        ],
        space=pltpu.HBM,
    )
    field = pltpu.VMEM((3 * count, 3 * feature_count, size), BF16)
    first = call(
        functools.partial(first_kernel, owners),
        jax.ShapeDtypeStruct(features.shape, F32),
        scalars,
        [features, near_one, far_one, tiles],
        [field],
    )
    line = [packed] + [send(packed, m) for m in (8, 16, 24)]
    column = jnp.stack(line)
    near_two, far_two = send(first, replicas), far(first)
    across_x, across_y = send(column, 4), send(column[0:3], 2)
    corner_one = send(across_y, 4)
    corner_two = send(jnp.concatenate([column[3:4], across_x[3:4]]), 2)
    mine, other = call(
        functools.partial(second_kernel, owners),
        tuple(jax.ShapeDtypeStruct((feature_count, half), F32) for _ in range(2)),
        scalars,
        [first, near_two, far_two, tiles, features, rank_row],
        [field],
    )
    own = jnp.stack([mine, send(other, 1), send(mine, 2), send(other, 3)])
    facing = send(own, 4)
    ring = [send(own, m) for m in (24, 16)]
    near_line = send(own, 8)
    mid_rows = hidden // owners
    begun = call(
        functools.partial(forward_kernel, mid_rows),
        (
            jax.ShapeDtypeStruct((3 * half, mid_rows), BF16),
            jax.ShapeDtypeStruct((3 * half, hidden), BF16),
            jax.ShapeDtypeStruct((3 * half, hidden), F32),
            jax.ShapeDtypeStruct((3 * half, hidden), F32),
        ),
        [place],
        [own, facing, near_line, w_in, w_mid],
        micros=3.7,
        mib=20,
    )
    orders = ((0, 4, 8, 12), (2, 6, 10, 14), (1, 5, 9), (3, 7, 11), (13, 15))
    arranged, slot_rows = call(
        functools.partial(cotangent_kernel, orders, classes, segment),
        (
            jax.ShapeDtypeStruct((owners, half, classes), BF16),
            jax.ShapeDtypeStruct((owners, 1, half), F32),
        ),
        [place],
        [column, across_x, across_y, corner_one, corner_two],
        [
            pltpu.VMEM((devices // 2, classes, width), BF16),
            pltpu.VMEM((devices // 2, rows, width), F32),
        ],
    )
    near_ready, *begun = lax.optimization_barrier((near_line, *begun))
    near_across = send(near_ready, 4)
    *ring, gate, slot_rows = lax.optimization_barrier((*ring, begun[0], slot_rows))
    begun = (gate, *begun[1:])
    last = send(jnp.stack(ring), 4)

    feats = feature_count * replicas
    mid_shape = jax.ShapeDtypeStruct((mid_rows, hidden), F32)
    out_shape = jax.ShapeDtypeStruct((classes, hidden), F32)
    grads_shape = jax.ShapeDtypeStruct((mid_rows + classes, hidden), F32)
    in_shape = jax.ShapeDtypeStruct((feats, hidden), F32)
    batch_shape = jax.ShapeDtypeStruct((feats, width), F32)

    def train(before, sources, masks, states, finish, mib):
        fresh = half * (len(masks) - 3 * bool(states))
        rows = half * len(masks)
        rest = (
            (in_shape,)
            if finish
            else (
                jax.ShapeDtypeStruct((feats, rows), BF16),
                jax.ShapeDtypeStruct((rows, hidden), BF16),
                jax.ShapeDtypeStruct((rows, hidden), F32),
            )
        )
        return call(
            functools.partial(train_kernel, fresh, masks, bool(states), bool(before), finish),
            (grads_shape, batch_shape, *rest),
            [place],
            [*before, *sources, *states, arranged, slot_rows, w_in, w_mid, w_out],
            micros=2.5 * len(masks),
            mib=mib,
        )

    grads_before, batch_before, in_before = train(
        (), [own, facing, near_line, *ring], (0, 1, 2, 6, 4), begun, True, 32
    )
    grads, batch_features, *rest = train(
        (grads_before, batch_before), [near_across, last[0], last[1]], (3, 7, 5), (), False, 20
    )
    theirs = send(grads, 1)
    grad_in = call(last_kernel, in_shape, [], [in_before, *rest, w_mid], micros=2.5, mib=12)
    their_in = send(grad_in, 1)
    grad_mid, grad_out = call(
        functools.partial(add_kernel, True), (mid_shape, out_shape), [], [grads, theirs]
    )
    their_in, grad_mid = lax.optimization_barrier((their_in, grad_mid))
    grad_in = call(functools.partial(add_kernel, False), (in_shape,), [], [grad_in, their_in])[0]
    return batch_features, grad_in, grad_mid, grad_out


def extended_2(cells, sides, width):
    for axis, dim in sides:
        count = lax.axis_size(axis)
        head = lax.slice_in_dim(cells, 0, width, axis=dim)
        tail = lax.slice_in_dim(cells, cells.shape[dim] - width, cells.shape[dim], axis=dim)
        cells = jnp.concatenate(
            [
                lax.ppermute(tail, axis, [(i, (i + 1) % count) for i in range(count)]),
                cells,
                lax.ppermute(head, axis, [((i + 1) % count, i) for i in range(count)]),
            ],
            axis=dim,
        )
    return cells


def silu_slope(pre):
    sigma = jax.nn.sigmoid(pre)
    return sigma * (1.0 + pre * (1.0 - sigma))


def neighbour_blocks(local, margin, tile_size):
    extended = extended_2(local, (("dom", 1),), margin * tile_size)
    return extended


def apply_operator(local, tiles_across, assignment_map, relative, margin):
    feature_count, node_count = local.shape
    tile_size = tiles_across.shape[1]
    extended = neighbour_blocks(local, margin, tile_size)
    blocks = extended.reshape(feature_count, -1, tile_size)
    input_values = jnp.take(blocks, relative, axis=1)
    block_products = jnp.einsum(
        "lkz,glz->glk", tiles_across, input_values, precision=lax.Precision.HIGHEST
    )
    final_result = jnp.einsum(
        "wy,kya->kwa", assignment_map, block_products, precision=lax.Precision.HIGHEST
    )
    return final_result.reshape(feature_count, node_count)


def split_plan(
    features, tiles, tile_row, tile_col, tile_count, dest_slot, w_in, w_mid, w_out, cotangent
):
    node_partition = lax.axis_index("dom")
    owners = lax.axis_size("dom")
    replicas = lax.axis_size("rep")
    feature_count, node_count = features.shape
    capacity = tiles.shape[0]
    tile_size = tiles.shape[1]
    block_count = node_count // tile_size
    total_blocks = block_count * owners
    relative = jnp.mod(tile_col - node_partition * block_count + block_count, total_blocks)
    live_mask = (jnp.arange(capacity, dtype=jnp.int32) < tile_count[0]).astype(jnp.float32)
    assignment_map = (
        tile_row[None, :] == jnp.arange(block_count, dtype=jnp.int32)[:, None]
    ).astype(jnp.float32) * live_mask[None, :]
    tiles_across = tiles.astype(jnp.float32)
    first = apply_operator(features, tiles_across, assignment_map, relative, block_count)
    second = (
        2.0 * apply_operator(first, tiles_across, assignment_map, relative, block_count) - features
    )
    diffused = series_zero * features + series_one * first + series_two * second
    segment = node_count // (owners * replicas)
    batch_rows = node_count // replicas
    sort_order = jnp.argsort(dest_slot)
    sorted_slots = jnp.take(dest_slot, sort_order)
    moved_rows = jnp.take(diffused, sort_order, axis=1).reshape(
        feature_count, owners, replicas, segment
    )
    moved_slots = sorted_slots.astype(jnp.float32).reshape(1, owners, replicas, segment)
    arrived, arrived_slots = (
        lax.all_to_all(
            lax.all_to_all(moved_rows, "dom", split_axis=1, concat_axis=1, tiled=True),
            "rep",
            split_axis=2,
            concat_axis=0,
            tiled=True,
        ),
        lax.all_to_all(
            lax.all_to_all(moved_slots, "dom", split_axis=1, concat_axis=1, tiled=True),
            "rep",
            split_axis=2,
            concat_axis=0,
            tiled=True,
        ),
    )
    owner_index = node_partition * replicas + lax.axis_index("rep")
    local_slots = arrived_slots[0].reshape(-1).astype(jnp.int32) - owner_index * batch_rows
    gathered = arrived.reshape(feature_count * replicas, -1)
    batch_features = jnp.zeros(gathered.shape, jnp.float32).at[:, local_slots].set(gathered)
    inputs_bf = batch_features.astype(jnp.bfloat16)
    pre_one = lax.dot_general(inputs_bf, w_in, LEADING, preferred_element_type=jnp.float32)
    hidden_one = jax.nn.silu(pre_one).astype(jnp.bfloat16)
    pre_two = jnp.dot(hidden_one, w_mid, preferred_element_type=jnp.float32)
    hidden_two = jax.nn.silu(pre_two).astype(jnp.bfloat16)
    grad_out = jnp.dot(cotangent, hidden_two, preferred_element_type=jnp.float32)
    back_two = lax.dot_general(cotangent, w_out, LEADING, preferred_element_type=jnp.float32)
    delta_two = (back_two * silu_slope(pre_two)).astype(jnp.bfloat16)
    back_one = lax.dot_general(delta_two, w_mid, TRAILING, preferred_element_type=jnp.float32)
    delta_one = (back_one * silu_slope(pre_one)).astype(jnp.bfloat16)
    grad_in = jnp.dot(inputs_bf, delta_one, preferred_element_type=jnp.float32)
    mid_shard = lax.psum_scatter(
        lax.dot_general(hidden_one, delta_two, LEADING, preferred_element_type=jnp.float32),
        "dom",
        scatter_dimension=0,
        tiled=True,
    )
    grad_mid = lax.psum(mid_shard, "rep")
    grad_in, grad_out = lax.psum((grad_in, grad_out), ("dom", "rep"))
    return (batch_features, grad_in, grad_mid, grad_out)


def solution(mesh):
    compact = mesh.shape["dom"] == 8 and mesh.shape["rep"] == 4
    shards = gathered_plan if compact else split_plan
    in_specs = (
        P("rep", "dom"),
        P("dom", None, None),
        P("dom"),
        P("dom"),
        P("dom"),
        P("dom"),
        P(),
        P(),
        P(),
        P(None, ("dom", "rep")),
    )
    out_specs = (P(None, ("dom", "rep")), P(), P("dom", None), P())
    return jax.shard_map(shards, mesh=mesh, in_specs=in_specs, out_specs=out_specs, check_vma=False)
```

```python
import functools

import jax
import jax.numpy as jnp
from jax import lax
from jax.experimental import pallas as pl
from jax.experimental.pallas import tpu as pltpu
from jax.sharding import PartitionSpec as P

series_zero = 0.3085083
series_one = -0.4305395
series_two = 0.1864784
LEADING = (((0,), (0,)), ((), ()))
TRAILING = (((1,), (1,)), ((), ()))
AXES = ("dom", "rep")
F32 = jnp.float32
BF16 = jnp.bfloat16
VMEM = pl.BlockSpec(memory_space=pltpu.VMEM)
SMEM = pl.BlockSpec(memory_space=pltpu.SMEM)


def pieces(value):
    high = value.astype(BF16)
    rest = value - high.astype(F32)
    middle = rest.astype(BF16)
    low = (rest - middle.astype(F32)).astype(BF16)
    return jnp.concatenate([high, middle, low], axis=0)


def whole(parts):
    rows = parts.shape[0] // 3
    return parts[:rows] + parts[rows : 2 * rows] + parts[2 * rows :]


def open_kernel(place, out):
    out[...] = jnp.full(out.shape, place[0], F32)


def prepare_kernel(segment, block, place, slots, cot, opened, packed, rank_row):
    nodes = slots.shape[1]
    half = nodes // 2
    row = slots[...].astype(F32)
    column = jnp.broadcast_to(row, (8, nodes)).T[:, 0:1]
    wide = jnp.broadcast_to(row, (nodes, nodes))
    order = jnp.sum(jnp.where(column < wide, 1.0, 0.0), axis=0, keepdims=True).astype(jnp.int32)
    target = slots[...] // block
    rank = (target % 2) * half + (target // 2) * segment + order - target * segment
    rank_row[...] = rank
    rank_column = jnp.broadcast_to(rank.astype(F32), (8, nodes)).T[:, 0:1]
    lane = lax.broadcasted_iota(jnp.int32, (nodes, nodes), 1).astype(F32)
    ordered = jnp.sum(jnp.where(rank_column == lane, column, 0.0), axis=0, keepdims=True)
    mine = jnp.where(place[1] % 2 == 0, ordered[:, :half], ordered[:, half:])
    classes, width = cot.shape
    packed[0:classes, :] = cot[...].astype(F32)
    extra = packed.shape[0] - classes
    rows = half // width
    for index in range(rows):
        packed[classes + index : classes + index + 1, :] = mine[:, index * width : (index + 1) * width]
    if extra > rows:
        packed[classes + rows :, :] = jnp.zeros((extra - rows, width), F32)


def operate(place, live, row, col, own, near, far, tiles, field, owners):
    capacity, size, _ = tiles.shape
    count = own.shape[1] // size
    dom = place[0]
    odd = dom % 2
    near_base = (1 - odd) * 2 * count
    far_base = odd * 2 * count
    for index in range(count):
        cut = slice(index * size, (index + 1) * size)
        field[count + index] = pieces(own[:, cut])
        field[near_base + index] = pieces(near[:, cut])
        field[far_base + index] = pieces(far[:, cut])
    total = count * owners
    sums = [jnp.zeros((own.shape[0], size), F32) for _ in range(count)]
    for slot in range(capacity):
        relative = lax.rem(col[slot] - dom * count + count + total, total)
        target = jnp.where(slot < live[0], row[slot], -1)
        product = whole(
            lax.dot_general(field[relative], tiles[slot], TRAILING, preferred_element_type=F32)
        )
        for index in range(count):
            sums[index] = sums[index] + jnp.where(target == index, product, 0.0)
    return jnp.concatenate(sums, axis=1)


def first_kernel(owners, place, live, row, col, own, near, far, tiles, first, field):
    first[...] = operate(place, live, row, col, own, near, far, tiles, field, owners)


def second_kernel(
    owners, place, live, row, col, own, near, far, tiles, features, rank_row, mine, other, field
):
    applied = operate(place, live, row, col, own, near, far, tiles, field, owners)
    base = features[...]
    second = 2.0 * applied - base
    diffused = series_zero * base + series_one * own[...] + series_two * second
    nodes = base.shape[1]
    spot = lax.broadcasted_iota(jnp.int32, (nodes, nodes), 0)
    chosen = jnp.where(spot == rank_row[...], 1.0, 0.0).astype(BF16)
    ordered = whole(lax.dot_general(pieces(diffused), chosen, TRAILING, preferred_element_type=F32))
    low, high = ordered[:, : nodes // 2], ordered[:, nodes // 2 :]
    core = place[1] % 2
    mine[...] = jnp.where(core == 0, low, high)
    other[...] = jnp.where(core == 0, high, low)


def cotangent_kernel(orders, classes, segment, place, *refs):
    sources = refs[: len(orders)]
    arranged, slot_rows, held, listed = refs[len(orders) :]
    me = place[0] * 2 + place[1] // 2
    core = place[1] % 2
    blocks = held.shape[0]
    width = held.shape[2]
    parts = arranged.shape[0]
    rows = listed.shape[1]
    for source, order in zip(sources, orders):
        for index, mask in enumerate(order):
            block = jnp.bitwise_xor(me, mask)
            held[block] = source[index, 0:classes, :].astype(BF16)
            listed[block] = source[index, classes : classes + rows, :]
    lists = []
    for part in range(parts):
        listing = listed[2 * part]
        row = jnp.concatenate([listing[i : i + 1] for i in range(rows)], axis=1)
        slot_rows[part] = row
        lists.append(row)
    columns = jnp.concatenate(lists, axis=0).T
    lane = lax.broadcasted_iota(jnp.int32, (segment, width), 1).astype(F32)
    for block in range(blocks):
        start = ((2 * block + core) * width).astype(F32)
        cut = slice(block * segment, (block + 1) * segment)
        chosen = jnp.concatenate(
            [
                jnp.where(columns[cut, part : part + 1] - start == lane, 1.0, 0.0)
                for part in range(parts)
            ],
            axis=0,
        ).astype(BF16)
        moved = lax.dot_general(chosen, held[block], TRAILING, preferred_element_type=F32)
        for part in range(parts):
            arranged[part, cut, :] = moved[part * segment : (part + 1) * segment].astype(BF16)


def activated(pre):
    gate = 0.5 * jnp.tanh(0.5 * pre) + 0.5
    value = pre * gate
    return value.astype(BF16), gate + value * (1.0 - gate)


def feature_rows(source, rep):
    replicas = source.shape[0]
    return jnp.concatenate([source[jnp.bitwise_xor(rep, i)] for i in range(replicas)], axis=0)


def forward(inputs, dom, mid_rows, w_in, w_mid):
    pre_one = lax.dot_general(inputs, w_in[...], LEADING, preferred_element_type=F32)
    hidden_one, slope_one = activated(pre_one)
    own_pre = lax.dot_general(
        inputs,
        w_in[:, pl.ds(pl.multiple_of(dom * mid_rows, mid_rows), mid_rows)],
        LEADING,
        preferred_element_type=F32,
    )
    own_hidden, _ = activated(own_pre)
    pre_two = jnp.dot(hidden_one, w_mid[...], preferred_element_type=F32)
    hidden_two, slope_two = activated(pre_two)
    return own_hidden, hidden_two, slope_one, slope_two


def forward_kernel(mid_rows, place, *refs):
    *sources, w_in, w_mid, own_hidden, hidden_two, slope_one, slope_two = refs
    dom, rep = place[0], place[1]
    values = [feature_rows(source, rep).astype(BF16) for source in sources]
    results = forward(jnp.concatenate(values, axis=1), dom, mid_rows, w_in, w_mid)
    for out, result in zip((own_hidden, hidden_two, slope_one, slope_two), results):
        out[...] = result


def train_kernel(fresh, masks, begun, again, finish, place, *refs):
    if again:
        grads_before, batch_before = refs[:2]
        refs = refs[2:]
    sources = refs[: len(masks)]
    refs = refs[len(masks) :]
    states = refs[:4] if begun else ()
    arranged, slot_rows, w_in, w_mid, w_out, grads, batch, *rest = refs[len(states) :]
    mid_rows = grads.shape[0] - arranged.shape[2]
    dom, rep = place[0], place[1]
    width = batch.shape[1]
    replicas = sources[0].shape[0]
    own_start = (dom * replicas + rep) * width
    values, cots = [], []
    moved = batch_before[...] if again else jnp.zeros(batch.shape, F32)
    for source, mask in zip(sources, masks):
        part = jnp.bitwise_xor(dom, mask)
        value = feature_rows(source, rep)
        spot = lax.broadcasted_iota(jnp.int32, (width, value.shape[1]), 0) + own_start
        chosen = jnp.where(spot.astype(F32) == slot_rows[part], 1.0, 0.0).astype(BF16)
        moved = moved + whole(
            lax.dot_general(pieces(value), chosen, TRAILING, preferred_element_type=F32)
        )
        values.append(value.astype(BF16))
        cots.append(arranged[part])
    batch[...] = moved
    inputs = jnp.concatenate(values, axis=1)
    cot = jnp.concatenate(cots, axis=0)
    done = inputs.shape[1] - fresh
    results = forward(inputs[:, done:], dom, mid_rows, w_in, w_mid)
    if begun:
        results = [
            jnp.concatenate([state[...], result], axis=0) for state, result in zip(states, results)
        ]
    own_hidden, hidden_two, slope_one, slope_two = results
    term = lax.dot_general(cot, hidden_two, LEADING, preferred_element_type=F32)
    grads[mid_rows:, :] = grads_before[mid_rows:, :] + term if again else term
    back_two = jnp.dot(cot, w_out[...], preferred_element_type=F32)
    delta_two = (back_two * slope_two).astype(BF16)
    term = lax.dot_general(own_hidden, delta_two, LEADING, preferred_element_type=F32)
    grads[:mid_rows, :] = grads_before[:mid_rows, :] + term if again else term
    if finish:
        rest[0][...] = input_gradient(inputs, delta_two, slope_one, w_mid)
    else:
        for out, value in zip(rest, (inputs, delta_two, slope_one)):
            out[...] = value


def input_gradient(inputs, delta_two, slope_one, w_mid):
    back_one = lax.dot_general(delta_two, w_mid[...], TRAILING, preferred_element_type=F32)
    delta_one = (back_one * slope_one).astype(BF16)
    return jnp.dot(inputs, delta_one, preferred_element_type=F32)


def last_kernel(before, inputs, delta_two, slope_one, w_mid, grad_in):
    grad_in[...] = before[...] + input_gradient(
        inputs[...], delta_two[...], slope_one[...], w_mid
    )


def add_kernel(split, mine, theirs, *outs):
    start = 0
    for out in outs:
        cut = slice(start, start + out.shape[0]) if split else slice(None)
        out[...] = mine[cut, :] + theirs[cut, :]
        start += out.shape[0]


def call(kernel, outs, scalars, arrays, scratch=(), micros=1.5, mib=16):
    cost = pl.CostEstimate(
        flops=int(micros * 1e9), bytes_accessed=int(micros * 3.6e6), transcendentals=0
    )
    return pl.pallas_call(
        kernel,
        out_shape=outs,
        in_specs=[SMEM] * len(scalars) + [VMEM] * len(arrays),
        out_specs=jax.tree.map(lambda _: VMEM, outs),
        scratch_shapes=list(scratch),
        compiler_params=pltpu.CompilerParams(vmem_limit_bytes=mib * 2**20),
        cost_estimate=cost,
    )(*scalars, *arrays)


def exchanged(value, mask, devices):
    return lax.ppermute(value, AXES, [(i, i ^ mask) for i in range(devices)])


def gathered_plan(
    features, tiles, tile_row, tile_col, tile_count, dest_slot, w_in, w_mid, w_out, cotangent
):
    owners, replicas = lax.axis_size("dom"), lax.axis_size("rep")
    devices = owners * replicas
    place = jnp.stack([lax.axis_index("dom"), lax.axis_index("rep")]).astype(jnp.int32)
    scalars = [place, tile_count, tile_row, tile_col]
    feature_count, node_count = features.shape
    size = tiles.shape[1]
    classes, width = cotangent.shape
    hidden = w_in.shape[1]
    segment = node_count // devices
    half = node_count // 2
    count = node_count // size
    send = functools.partial(exchanged, devices=devices)
    far_pairs = [
        (d * replicas + r, ((d + 1 if d % 2 else d - 1) % owners) * replicas + r)
        for d in range(owners)
        for r in range(replicas)
    ]

    def far(value):
        return lax.ppermute(value, AXES, far_pairs)

    rows = half // width
    padded = classes + rows + (-(classes + rows)) % 8
    opened = call(open_kernel, jax.ShapeDtypeStruct((8, 128), F32), [place], [], micros=4.0)
    near_one, far_one = send(features, replicas), far(features)
    packed, rank_row = call(
        functools.partial(prepare_kernel, segment, width),
        (
            jax.ShapeDtypeStruct((padded, width), F32),
            jax.ShapeDtypeStruct((1, node_count), jnp.int32),
        ),
        [place],
        [dest_slot.reshape(1, -1), cotangent, opened],
    )
    field = pltpu.VMEM((3 * count, 3 * feature_count, size), BF16)
    first = call(
        functools.partial(first_kernel, owners),
        jax.ShapeDtypeStruct(features.shape, F32),
        scalars,
        [features, near_one, far_one, tiles],
        [field],
    )
    line = [packed] + [send(packed, m) for m in (8, 16, 24)]
    column = jnp.stack(line)
    near_two, far_two = send(first, replicas), far(first)
    across_y, across_x = send(jnp.stack(line[0:3]), 2), send(column, 4)
    corner_one = send(across_y, 4)
    corner_two = send(jnp.concatenate([column[3:4], across_x[3:4]]), 2)
    mine, other = call(
        functools.partial(second_kernel, owners),
        tuple(jax.ShapeDtypeStruct((feature_count, half), F32) for _ in range(2)),
        scalars,
        [first, near_two, far_two, tiles, features, rank_row],
        [field],
    )
    own = jnp.stack([mine, send(other, 1), send(mine, 2), send(other, 3)])
    facing = send(own, 4)
    ring = [send(own, m) for m in (24, 16)]
    near_line = send(own, 8)
    mid_rows = hidden // owners
    begun = call(
        functools.partial(forward_kernel, mid_rows),
        (
            jax.ShapeDtypeStruct((3 * half, mid_rows), BF16),
            jax.ShapeDtypeStruct((3 * half, hidden), BF16),
            jax.ShapeDtypeStruct((3 * half, hidden), F32),
            jax.ShapeDtypeStruct((3 * half, hidden), F32),
        ),
        [place],
        [own, facing, near_line, w_in, w_mid],
        micros=3.7,
        mib=20,
    )
    orders = ((0, 4, 8, 12), (1, 5, 9), (2, 6, 10, 14), (3, 7, 11), (13, 15))
    arranged, slot_rows = call(
        functools.partial(cotangent_kernel, orders, classes, segment),
        (
            jax.ShapeDtypeStruct((owners, half, classes), BF16),
            jax.ShapeDtypeStruct((owners, 1, half), F32),
        ),
        [place],
        [column, across_y, across_x, corner_one, corner_two],
        [
            pltpu.VMEM((devices // 2, classes, width), BF16),
            pltpu.VMEM((devices // 2, rows, width), F32),
        ],
    )
    near_ready, *begun = lax.optimization_barrier((near_line, *begun))
    near_across = send(near_ready, 4)
    *ring, gate, slot_rows = lax.optimization_barrier((*ring, begun[0], slot_rows))
    begun = (gate, *begun[1:])
    last = send(jnp.stack(ring), 4)

    feats = feature_count * replicas
    mid_shape = jax.ShapeDtypeStruct((mid_rows, hidden), F32)
    out_shape = jax.ShapeDtypeStruct((classes, hidden), F32)
    grads_shape = jax.ShapeDtypeStruct((mid_rows + classes, hidden), F32)
    in_shape = jax.ShapeDtypeStruct((feats, hidden), F32)
    batch_shape = jax.ShapeDtypeStruct((feats, width), F32)

    def train(before, sources, masks, states, finish, mib):
        fresh = half * (len(masks) - 3 * bool(states))
        rows = half * len(masks)
        rest = (
            (in_shape,)
            if finish
            else (
                jax.ShapeDtypeStruct((feats, rows), BF16),
                jax.ShapeDtypeStruct((rows, hidden), BF16),
                jax.ShapeDtypeStruct((rows, hidden), F32),
            )
        )
        return call(
            functools.partial(train_kernel, fresh, masks, bool(states), bool(before), finish),
            (grads_shape, batch_shape, *rest),
            [place],
            [*before, *sources, *states, arranged, slot_rows, w_in, w_mid, w_out],
            micros=2.5 * len(masks),
            mib=mib,
        )

    grads_before, batch_before, in_before = train(
        (), [own, facing, near_line, *ring], (0, 1, 2, 6, 4), begun, True, 32
    )
    grads, batch_features, *rest = train(
        (grads_before, batch_before), [near_across, last[0], last[1]], (3, 7, 5), (), False, 20
    )
    theirs = send(grads, 1)
    grad_in = call(last_kernel, in_shape, [], [in_before, *rest, w_mid], micros=2.5, mib=12)
    their_in = send(grad_in, 1)
    grad_mid, grad_out = call(
        functools.partial(add_kernel, True), (mid_shape, out_shape), [], [grads, theirs]
    )
    their_in, grad_mid = lax.optimization_barrier((their_in, grad_mid))
    grad_in = call(functools.partial(add_kernel, False), (in_shape,), [], [grad_in, their_in])[0]
    return batch_features, grad_in, grad_mid, grad_out


def extended_2(cells, sides, width):
    for axis, dim in sides:
        count = lax.axis_size(axis)
        head = lax.slice_in_dim(cells, 0, width, axis=dim)
        tail = lax.slice_in_dim(cells, cells.shape[dim] - width, cells.shape[dim], axis=dim)
        cells = jnp.concatenate(
            [
                lax.ppermute(tail, axis, [(i, (i + 1) % count) for i in range(count)]),
                cells,
                lax.ppermute(head, axis, [((i + 1) % count, i) for i in range(count)]),
            ],
            axis=dim,
        )
    return cells


def silu_slope(pre):
    sigma = jax.nn.sigmoid(pre)
    return sigma * (1.0 + pre * (1.0 - sigma))


def neighbour_blocks(local, margin, tile_size):
    extended = extended_2(local, (("dom", 1),), margin * tile_size)
    return extended


def apply_operator(local, tiles_across, assignment_map, relative, margin):
    feature_count, node_count = local.shape
    tile_size = tiles_across.shape[1]
    extended = neighbour_blocks(local, margin, tile_size)
    blocks = extended.reshape(feature_count, -1, tile_size)
    input_values = jnp.take(blocks, relative, axis=1)
    block_products = jnp.einsum(
        "lkz,glz->glk", tiles_across, input_values, precision=lax.Precision.HIGHEST
    )
    final_result = jnp.einsum(
        "wy,kya->kwa", assignment_map, block_products, precision=lax.Precision.HIGHEST
    )
    return final_result.reshape(feature_count, node_count)


def split_plan(
    features, tiles, tile_row, tile_col, tile_count, dest_slot, w_in, w_mid, w_out, cotangent
):
    node_partition = lax.axis_index("dom")
    owners = lax.axis_size("dom")
    replicas = lax.axis_size("rep")
    feature_count, node_count = features.shape
    capacity = tiles.shape[0]
    tile_size = tiles.shape[1]
    block_count = node_count // tile_size
    total_blocks = block_count * owners
    relative = jnp.mod(tile_col - node_partition * block_count + block_count, total_blocks)
    live_mask = (jnp.arange(capacity, dtype=jnp.int32) < tile_count[0]).astype(jnp.float32)
    assignment_map = (
        tile_row[None, :] == jnp.arange(block_count, dtype=jnp.int32)[:, None]
    ).astype(jnp.float32) * live_mask[None, :]
    tiles_across = tiles.astype(jnp.float32)
    first = apply_operator(features, tiles_across, assignment_map, relative, block_count)
    second = (
        2.0 * apply_operator(first, tiles_across, assignment_map, relative, block_count) - features
    )
    diffused = series_zero * features + series_one * first + series_two * second
    segment = node_count // (owners * replicas)
    batch_rows = node_count // replicas
    sort_order = jnp.argsort(dest_slot)
    sorted_slots = jnp.take(dest_slot, sort_order)
    moved_rows = jnp.take(diffused, sort_order, axis=1).reshape(
        feature_count, owners, replicas, segment
    )
    moved_slots = sorted_slots.astype(jnp.float32).reshape(1, owners, replicas, segment)
    arrived, arrived_slots = (
        lax.all_to_all(
            lax.all_to_all(moved_rows, "dom", split_axis=1, concat_axis=1, tiled=True),
            "rep",
            split_axis=2,
            concat_axis=0,
            tiled=True,
        ),
        lax.all_to_all(
            lax.all_to_all(moved_slots, "dom", split_axis=1, concat_axis=1, tiled=True),
            "rep",
            split_axis=2,
            concat_axis=0,
            tiled=True,
        ),
    )
    owner_index = node_partition * replicas + lax.axis_index("rep")
    local_slots = arrived_slots[0].reshape(-1).astype(jnp.int32) - owner_index * batch_rows
    gathered = arrived.reshape(feature_count * replicas, -1)
    batch_features = jnp.zeros(gathered.shape, jnp.float32).at[:, local_slots].set(gathered)
    inputs_bf = batch_features.astype(jnp.bfloat16)
    pre_one = lax.dot_general(inputs_bf, w_in, LEADING, preferred_element_type=jnp.float32)
    hidden_one = jax.nn.silu(pre_one).astype(jnp.bfloat16)
    pre_two = jnp.dot(hidden_one, w_mid, preferred_element_type=jnp.float32)
    hidden_two = jax.nn.silu(pre_two).astype(jnp.bfloat16)
    grad_out = jnp.dot(cotangent, hidden_two, preferred_element_type=jnp.float32)
    back_two = lax.dot_general(cotangent, w_out, LEADING, preferred_element_type=jnp.float32)
    delta_two = (back_two * silu_slope(pre_two)).astype(jnp.bfloat16)
    back_one = lax.dot_general(delta_two, w_mid, TRAILING, preferred_element_type=jnp.float32)
    delta_one = (back_one * silu_slope(pre_one)).astype(jnp.bfloat16)
    grad_in = jnp.dot(inputs_bf, delta_one, preferred_element_type=jnp.float32)
    mid_shard = lax.psum_scatter(
        lax.dot_general(hidden_one, delta_two, LEADING, preferred_element_type=jnp.float32),
        "dom",
        scatter_dimension=0,
        tiled=True,
    )
    grad_mid = lax.psum(mid_shard, "rep")
    grad_in, grad_out = lax.psum((grad_in, grad_out), ("dom", "rep"))
    return (batch_features, grad_in, grad_mid, grad_out)


def solution(mesh):
    compact = mesh.shape["dom"] == 8 and mesh.shape["rep"] == 4
    shards = gathered_plan if compact else split_plan
    in_specs = (
        P("rep", "dom"),
        P("dom", None, None),
        P("dom"),
        P("dom"),
        P("dom"),
        P("dom"),
        P(),
        P(),
        P(),
        P(None, ("dom", "rep")),
    )
    out_specs = (P(None, ("dom", "rep")), P(), P("dom", None), P())
    return jax.shard_map(shards, mesh=mesh, in_specs=in_specs, out_specs=out_specs, check_vma=False)
```

```python
import functools

import jax
import jax.numpy as jnp
from jax import lax
from jax.experimental import pallas as pl
from jax.experimental.pallas import tpu as pltpu
from jax.sharding import PartitionSpec as P

series_zero = 0.3085083
series_one = -0.4305395
series_two = 0.1864784
LEADING = (((0,), (0,)), ((), ()))
TRAILING = (((1,), (1,)), ((), ()))
AXES = ("dom", "rep")
F32 = jnp.float32
BF16 = jnp.bfloat16
VMEM = pl.BlockSpec(memory_space=pltpu.VMEM)
SMEM = pl.BlockSpec(memory_space=pltpu.SMEM)


def pieces(value):
    high = value.astype(BF16)
    rest = value - high.astype(F32)
    middle = rest.astype(BF16)
    low = (rest - middle.astype(F32)).astype(BF16)
    return jnp.concatenate([high, middle, low], axis=0)


def whole(parts):
    rows = parts.shape[0] // 3
    return parts[:rows] + parts[rows : 2 * rows] + parts[2 * rows :]


def open_kernel(place, out):
    out[...] = jnp.full(out.shape, place[0], F32)


def prepare_kernel(segment, block, place, slots, cot, opened, packed, rank_row):
    nodes = slots.shape[1]
    half = nodes // 2
    row = slots[...].astype(F32)
    column = jnp.broadcast_to(row, (8, nodes)).T[:, 0:1]
    wide = jnp.broadcast_to(row, (nodes, nodes))
    order = jnp.sum(jnp.where(column < wide, 1.0, 0.0), axis=0, keepdims=True).astype(jnp.int32)
    target = slots[...] // block
    rank = (target % 2) * half + (target // 2) * segment + order - target * segment
    rank_row[...] = rank
    rank_column = jnp.broadcast_to(rank.astype(F32), (8, nodes)).T[:, 0:1]
    lane = lax.broadcasted_iota(jnp.int32, (nodes, nodes), 1).astype(F32)
    ordered = jnp.sum(jnp.where(rank_column == lane, column, 0.0), axis=0, keepdims=True)
    mine = jnp.where(place[1] % 2 == 0, ordered[:, :half], ordered[:, half:])
    classes, width = cot.shape
    packed[0:classes, :] = cot[...].astype(F32)
    extra = packed.shape[0] - classes
    rows = half // width
    for index in range(rows):
        packed[classes + index : classes + index + 1, :] = mine[:, index * width : (index + 1) * width]
    if extra > rows:
        packed[classes + rows :, :] = jnp.zeros((extra - rows, width), F32)


def operate(place, live, row, col, own, near, far, tiles, field, sums, owners):
    capacity, size, _ = tiles.shape
    count = own.shape[1] // size
    dom = place[0]
    odd = dom % 2
    near_base = (1 - odd) * 2 * count
    far_base = odd * 2 * count
    for index in range(count):
        cut = slice(index * size, (index + 1) * size)
        field[count + index] = pieces(own[:, cut])
        field[near_base + index] = pieces(near[:, cut])
        field[far_base + index] = pieces(far[:, cut])
    total = count * owners
    sums[...] = jnp.zeros_like(sums)
    for slot in range(capacity):
        relative = lax.rem(col[slot] - dom * count + count + total, total)
        product = whole(
            lax.dot_general(field[relative], tiles[slot], TRAILING, preferred_element_type=F32)
        )
        sums[row[slot]] += jnp.where(slot < live[0], product, 0.0)
    return jnp.concatenate([sums[index] for index in range(count)], axis=1)


def first_kernel(owners, place, live, row, col, own, near, far, tiles, first, field, sums):
    first[...] = operate(place, live, row, col, own, near, far, tiles, field, sums, owners)


def second_kernel(
    owners, place, live, row, col, own, near, far, tiles, features, rank_row, mine, other, field, sums
):
    applied = operate(place, live, row, col, own, near, far, tiles, field, sums, owners)
    base = features[...]
    second = 2.0 * applied - base
    diffused = series_zero * base + series_one * own[...] + series_two * second
    nodes = base.shape[1]
    spot = lax.broadcasted_iota(jnp.int32, (nodes, nodes), 0)
    chosen = jnp.where(spot == rank_row[...], 1.0, 0.0).astype(BF16)
    ordered = whole(lax.dot_general(pieces(diffused), chosen, TRAILING, preferred_element_type=F32))
    low, high = ordered[:, : nodes // 2], ordered[:, nodes // 2 :]
    core = place[1] % 2
    mine[...] = jnp.where(core == 0, low, high)
    other[...] = jnp.where(core == 0, high, low)


def cotangent_kernel(orders, classes, segment, place, *refs):
    sources = refs[: len(orders)]
    arranged, slot_rows, held, listed = refs[len(orders) :]
    me = place[0] * 2 + place[1] // 2
    core = place[1] % 2
    blocks = held.shape[0]
    width = held.shape[2]
    parts = arranged.shape[0]
    rows = listed.shape[1]
    for source, order in zip(sources, orders):
        for index, mask in enumerate(order):
            block = jnp.bitwise_xor(me, mask)
            held[block] = source[index, 0:classes, :].astype(BF16)
            listed[block] = source[index, classes : classes + rows, :]
    lists = []
    for part in range(parts):
        listing = listed[2 * part]
        row = jnp.concatenate([listing[i : i + 1] for i in range(rows)], axis=1)
        slot_rows[part] = row
        lists.append(row)
    columns = jnp.concatenate(lists, axis=0).T
    lane = lax.broadcasted_iota(jnp.int32, (segment, width), 1).astype(F32)
    for block in range(blocks):
        start = ((2 * block + core) * width).astype(F32)
        cut = slice(block * segment, (block + 1) * segment)
        chosen = jnp.concatenate(
            [
                jnp.where(columns[cut, part : part + 1] - start == lane, 1.0, 0.0)
                for part in range(parts)
            ],
            axis=0,
        ).astype(BF16)
        moved = lax.dot_general(chosen, held[block], TRAILING, preferred_element_type=F32)
        for part in range(parts):
            arranged[part, cut, :] = moved[part * segment : (part + 1) * segment].astype(BF16)


def activated(pre):
    gate = 0.5 * jnp.tanh(0.5 * pre) + 0.5
    value = pre * gate
    return value.astype(BF16), gate + value * (1.0 - gate)


def feature_rows(source, rep):
    replicas = source.shape[0]
    return jnp.concatenate([source[jnp.bitwise_xor(rep, i)] for i in range(replicas)], axis=0)


def forward(inputs, dom, mid_rows, w_in, w_mid):
    pre_one = lax.dot_general(inputs, w_in[...], LEADING, preferred_element_type=F32)
    hidden_one, slope_one = activated(pre_one)
    own_pre = lax.dot_general(
        inputs,
        w_in[:, pl.ds(pl.multiple_of(dom * mid_rows, mid_rows), mid_rows)],
        LEADING,
        preferred_element_type=F32,
    )
    own_hidden, _ = activated(own_pre)
    pre_two = jnp.dot(hidden_one, w_mid[...], preferred_element_type=F32)
    hidden_two, slope_two = activated(pre_two)
    return own_hidden, hidden_two, slope_one, slope_two


def forward_kernel(mid_rows, place, *refs):
    *sources, w_in, w_mid, own_hidden, hidden_two, slope_one, slope_two = refs
    dom, rep = place[0], place[1]
    values = [feature_rows(source, rep).astype(BF16) for source in sources]
    results = forward(jnp.concatenate(values, axis=1), dom, mid_rows, w_in, w_mid)
    for out, result in zip((own_hidden, hidden_two, slope_one, slope_two), results):
        out[...] = result


def train_kernel(fresh, masks, begun, again, finish, place, *refs):
    if again:
        grads_before, batch_before = refs[:2]
        refs = refs[2:]
    sources = refs[: len(masks)]
    refs = refs[len(masks) :]
    states = refs[:4] if begun else ()
    arranged, slot_rows, w_in, w_mid, w_out, grads, batch, *rest = refs[len(states) :]
    mid_rows = grads.shape[0] - arranged.shape[2]
    dom, rep = place[0], place[1]
    width = batch.shape[1]
    replicas = sources[0].shape[0]
    own_start = (dom * replicas + rep) * width
    values, cots = [], []
    moved = batch_before[...] if again else jnp.zeros(batch.shape, F32)
    for source, mask in zip(sources, masks):
        part = jnp.bitwise_xor(dom, mask)
        value = feature_rows(source, rep)
        spot = lax.broadcasted_iota(jnp.int32, (width, value.shape[1]), 0) + own_start
        chosen = jnp.where(spot.astype(F32) == slot_rows[part], 1.0, 0.0).astype(BF16)
        moved = moved + whole(
            lax.dot_general(pieces(value), chosen, TRAILING, preferred_element_type=F32)
        )
        values.append(value.astype(BF16))
        cots.append(arranged[part])
    batch[...] = moved
    inputs = jnp.concatenate(values, axis=1)
    cot = jnp.concatenate(cots, axis=0)
    done = inputs.shape[1] - fresh
    results = forward(inputs[:, done:], dom, mid_rows, w_in, w_mid)
    if begun:
        results = [
            jnp.concatenate([state[...], result], axis=0) for state, result in zip(states, results)
        ]
    own_hidden, hidden_two, slope_one, slope_two = results
    term = lax.dot_general(cot, hidden_two, LEADING, preferred_element_type=F32)
    grads[mid_rows:, :] = grads_before[mid_rows:, :] + term if again else term
    back_two = jnp.dot(cot, w_out[...], preferred_element_type=F32)
    delta_two = (back_two * slope_two).astype(BF16)
    term = lax.dot_general(own_hidden, delta_two, LEADING, preferred_element_type=F32)
    grads[:mid_rows, :] = grads_before[:mid_rows, :] + term if again else term
    if finish:
        rest[0][...] = input_gradient(inputs, delta_two, slope_one, w_mid)
    else:
        for out, value in zip(rest, (inputs, delta_two, slope_one)):
            out[...] = value


def input_gradient(inputs, delta_two, slope_one, w_mid):
    back_one = lax.dot_general(delta_two, w_mid[...], TRAILING, preferred_element_type=F32)
    delta_one = (back_one * slope_one).astype(BF16)
    return jnp.dot(inputs, delta_one, preferred_element_type=F32)


def last_kernel(before, inputs, delta_two, slope_one, w_mid, grad_in):
    grad_in[...] = before[...] + input_gradient(
        inputs[...], delta_two[...], slope_one[...], w_mid
    )


def add_kernel(split, mine, theirs, *outs):
    start = 0
    for out in outs:
        cut = slice(start, start + out.shape[0]) if split else slice(None)
        out[...] = mine[cut, :] + theirs[cut, :]
        start += out.shape[0]


def call(kernel, outs, scalars, arrays, scratch=(), micros=1.5, mib=16):
    cost = pl.CostEstimate(
        flops=int(micros * 1e9), bytes_accessed=int(micros * 3.6e6), transcendentals=0
    )
    return pl.pallas_call(
        kernel,
        out_shape=outs,
        in_specs=[SMEM] * len(scalars) + [VMEM] * len(arrays),
        out_specs=jax.tree.map(lambda _: VMEM, outs),
        scratch_shapes=list(scratch),
        compiler_params=pltpu.CompilerParams(vmem_limit_bytes=mib * 2**20),
        cost_estimate=cost,
    )(*scalars, *arrays)


def exchanged(value, mask, devices):
    return lax.ppermute(value, AXES, [(i, i ^ mask) for i in range(devices)])


def gathered_plan(
    features, tiles, tile_row, tile_col, tile_count, dest_slot, w_in, w_mid, w_out, cotangent
):
    owners, replicas = lax.axis_size("dom"), lax.axis_size("rep")
    devices = owners * replicas
    place = jnp.stack([lax.axis_index("dom"), lax.axis_index("rep")]).astype(jnp.int32)
    scalars = [place, tile_count, tile_row, tile_col]
    feature_count, node_count = features.shape
    size = tiles.shape[1]
    classes, width = cotangent.shape
    hidden = w_in.shape[1]
    segment = node_count // devices
    half = node_count // 2
    count = node_count // size
    send = functools.partial(exchanged, devices=devices)
    far_pairs = [
        (d * replicas + r, ((d + 1 if d % 2 else d - 1) % owners) * replicas + r)
        for d in range(owners)
        for r in range(replicas)
    ]

    def far(value):
        return lax.ppermute(value, AXES, far_pairs)

    rows = half // width
    padded = classes + rows + (-(classes + rows)) % 8
    opened = call(open_kernel, jax.ShapeDtypeStruct((8, 128), F32), [place], [], micros=4.0)
    near_one, far_one = send(features, replicas), far(features)
    packed, rank_row = call(
        functools.partial(prepare_kernel, segment, width),
        (
            jax.ShapeDtypeStruct((padded, width), F32),
            jax.ShapeDtypeStruct((1, node_count), jnp.int32),
        ),
        [place],
        [dest_slot.reshape(1, -1), cotangent, opened],
    )
    field = pltpu.VMEM((3 * count, 3 * feature_count, size), BF16)
    sums = pltpu.VMEM((count, feature_count, size), F32)
    first = call(
        functools.partial(first_kernel, owners),
        jax.ShapeDtypeStruct(features.shape, F32),
        scalars,
        [features, near_one, far_one, tiles],
        [field, sums],
    )
    line = [packed] + [send(packed, m) for m in (8, 16, 24)]
    column = jnp.stack(line)
    near_two, far_two = send(first, replicas), far(first)
    across_y, across_x = send(jnp.stack(line[0:3]), 2), send(column, 4)
    corner_one = send(across_y, 4)
    corner_two = send(jnp.concatenate([column[3:4], across_x[3:4]]), 2)
    mine, other = call(
        functools.partial(second_kernel, owners),
        tuple(jax.ShapeDtypeStruct((feature_count, half), F32) for _ in range(2)),
        scalars,
        [first, near_two, far_two, tiles, features, rank_row],
        [field, sums],
    )
    own = jnp.stack([mine, send(other, 1), send(mine, 2), send(other, 3)])
    facing = send(own, 4)
    ring = [send(own, m) for m in (24, 16)]
    near_line = send(own, 8)
    mid_rows = hidden // owners
    begun = call(
        functools.partial(forward_kernel, mid_rows),
        (
            jax.ShapeDtypeStruct((3 * half, mid_rows), BF16),
            jax.ShapeDtypeStruct((3 * half, hidden), BF16),
            jax.ShapeDtypeStruct((3 * half, hidden), F32),
            jax.ShapeDtypeStruct((3 * half, hidden), F32),
        ),
        [place],
        [own, facing, near_line, w_in, w_mid],
        micros=3.7,
        mib=20,
    )
    orders = ((0, 4, 8, 12), (1, 5, 9), (2, 6, 10, 14), (3, 7, 11), (13, 15))
    arranged, slot_rows = call(
        functools.partial(cotangent_kernel, orders, classes, segment),
        (
            jax.ShapeDtypeStruct((owners, half, classes), BF16),
            jax.ShapeDtypeStruct((owners, 1, half), F32),
        ),
        [place],
        [column, across_y, across_x, corner_one, corner_two],
        [
            pltpu.VMEM((devices // 2, classes, width), BF16),
            pltpu.VMEM((devices // 2, rows, width), F32),
        ],
    )
    near_ready, *begun = lax.optimization_barrier((near_line, *begun))
    near_across = send(near_ready, 4)
    *ring, gate, slot_rows = lax.optimization_barrier((*ring, begun[0], slot_rows))
    begun = (gate, *begun[1:])
    last = send(jnp.stack(ring), 4)

    feats = feature_count * replicas
    mid_shape = jax.ShapeDtypeStruct((mid_rows, hidden), F32)
    out_shape = jax.ShapeDtypeStruct((classes, hidden), F32)
    grads_shape = jax.ShapeDtypeStruct((mid_rows + classes, hidden), F32)
    in_shape = jax.ShapeDtypeStruct((feats, hidden), F32)
    batch_shape = jax.ShapeDtypeStruct((feats, width), F32)

    def train(before, sources, masks, states, finish, mib):
        fresh = half * (len(masks) - 3 * bool(states))
        rows = half * len(masks)
        rest = (
            (in_shape,)
            if finish
            else (
                jax.ShapeDtypeStruct((feats, rows), BF16),
                jax.ShapeDtypeStruct((rows, hidden), BF16),
                jax.ShapeDtypeStruct((rows, hidden), F32),
            )
        )
        return call(
            functools.partial(train_kernel, fresh, masks, bool(states), bool(before), finish),
            (grads_shape, batch_shape, *rest),
            [place],
            [*before, *sources, *states, arranged, slot_rows, w_in, w_mid, w_out],
            micros=2.5 * len(masks),
            mib=mib,
        )

    grads_before, batch_before, in_before = train(
        (), [own, facing, near_line, *ring], (0, 1, 2, 6, 4), begun, True, 32
    )
    grads, batch_features, *rest = train(
        (grads_before, batch_before), [near_across, last[0], last[1]], (3, 7, 5), (), False, 20
    )
    theirs = send(grads, 1)
    grad_in = call(last_kernel, in_shape, [], [in_before, *rest, w_mid], micros=2.5, mib=12)
    their_in = send(grad_in, 1)
    grad_mid, grad_out = call(
        functools.partial(add_kernel, True), (mid_shape, out_shape), [], [grads, theirs]
    )
    their_in, grad_mid = lax.optimization_barrier((their_in, grad_mid))
    grad_in = call(functools.partial(add_kernel, False), (in_shape,), [], [grad_in, their_in])[0]
    return batch_features, grad_in, grad_mid, grad_out


def extended_2(cells, sides, width):
    for axis, dim in sides:
        count = lax.axis_size(axis)
        head = lax.slice_in_dim(cells, 0, width, axis=dim)
        tail = lax.slice_in_dim(cells, cells.shape[dim] - width, cells.shape[dim], axis=dim)
        cells = jnp.concatenate(
            [
                lax.ppermute(tail, axis, [(i, (i + 1) % count) for i in range(count)]),
                cells,
                lax.ppermute(head, axis, [((i + 1) % count, i) for i in range(count)]),
            ],
            axis=dim,
        )
    return cells


def silu_slope(pre):
    sigma = jax.nn.sigmoid(pre)
    return sigma * (1.0 + pre * (1.0 - sigma))


def neighbour_blocks(local, margin, tile_size):
    extended = extended_2(local, (("dom", 1),), margin * tile_size)
    return extended


def apply_operator(local, tiles_across, assignment_map, relative, margin):
    feature_count, node_count = local.shape
    tile_size = tiles_across.shape[1]
    extended = neighbour_blocks(local, margin, tile_size)
    blocks = extended.reshape(feature_count, -1, tile_size)
    input_values = jnp.take(blocks, relative, axis=1)
    block_products = jnp.einsum(
        "lkz,glz->glk", tiles_across, input_values, precision=lax.Precision.HIGHEST
    )
    final_result = jnp.einsum(
        "wy,kya->kwa", assignment_map, block_products, precision=lax.Precision.HIGHEST
    )
    return final_result.reshape(feature_count, node_count)


def split_plan(
    features, tiles, tile_row, tile_col, tile_count, dest_slot, w_in, w_mid, w_out, cotangent
):
    node_partition = lax.axis_index("dom")
    owners = lax.axis_size("dom")
    replicas = lax.axis_size("rep")
    feature_count, node_count = features.shape
    capacity = tiles.shape[0]
    tile_size = tiles.shape[1]
    block_count = node_count // tile_size
    total_blocks = block_count * owners
    relative = jnp.mod(tile_col - node_partition * block_count + block_count, total_blocks)
    live_mask = (jnp.arange(capacity, dtype=jnp.int32) < tile_count[0]).astype(jnp.float32)
    assignment_map = (
        tile_row[None, :] == jnp.arange(block_count, dtype=jnp.int32)[:, None]
    ).astype(jnp.float32) * live_mask[None, :]
    tiles_across = tiles.astype(jnp.float32)
    first = apply_operator(features, tiles_across, assignment_map, relative, block_count)
    second = (
        2.0 * apply_operator(first, tiles_across, assignment_map, relative, block_count) - features
    )
    diffused = series_zero * features + series_one * first + series_two * second
    segment = node_count // (owners * replicas)
    batch_rows = node_count // replicas
    sort_order = jnp.argsort(dest_slot)
    sorted_slots = jnp.take(dest_slot, sort_order)
    moved_rows = jnp.take(diffused, sort_order, axis=1).reshape(
        feature_count, owners, replicas, segment
    )
    moved_slots = sorted_slots.astype(jnp.float32).reshape(1, owners, replicas, segment)
    arrived, arrived_slots = (
        lax.all_to_all(
            lax.all_to_all(moved_rows, "dom", split_axis=1, concat_axis=1, tiled=True),
            "rep",
            split_axis=2,
            concat_axis=0,
            tiled=True,
        ),
        lax.all_to_all(
            lax.all_to_all(moved_slots, "dom", split_axis=1, concat_axis=1, tiled=True),
            "rep",
            split_axis=2,
            concat_axis=0,
            tiled=True,
        ),
    )
    owner_index = node_partition * replicas + lax.axis_index("rep")
    local_slots = arrived_slots[0].reshape(-1).astype(jnp.int32) - owner_index * batch_rows
    gathered = arrived.reshape(feature_count * replicas, -1)
    batch_features = jnp.zeros(gathered.shape, jnp.float32).at[:, local_slots].set(gathered)
    inputs_bf = batch_features.astype(jnp.bfloat16)
    pre_one = lax.dot_general(inputs_bf, w_in, LEADING, preferred_element_type=jnp.float32)
    hidden_one = jax.nn.silu(pre_one).astype(jnp.bfloat16)
    pre_two = jnp.dot(hidden_one, w_mid, preferred_element_type=jnp.float32)
    hidden_two = jax.nn.silu(pre_two).astype(jnp.bfloat16)
    grad_out = jnp.dot(cotangent, hidden_two, preferred_element_type=jnp.float32)
    back_two = lax.dot_general(cotangent, w_out, LEADING, preferred_element_type=jnp.float32)
    delta_two = (back_two * silu_slope(pre_two)).astype(jnp.bfloat16)
    back_one = lax.dot_general(delta_two, w_mid, TRAILING, preferred_element_type=jnp.float32)
    delta_one = (back_one * silu_slope(pre_one)).astype(jnp.bfloat16)
    grad_in = jnp.dot(inputs_bf, delta_one, preferred_element_type=jnp.float32)
    mid_shard = lax.psum_scatter(
        lax.dot_general(hidden_one, delta_two, LEADING, preferred_element_type=jnp.float32),
        "dom",
        scatter_dimension=0,
        tiled=True,
    )
    grad_mid = lax.psum(mid_shard, "rep")
    grad_in, grad_out = lax.psum((grad_in, grad_out), ("dom", "rep"))
    return (batch_features, grad_in, grad_mid, grad_out)


def solution(mesh):
    compact = mesh.shape["dom"] == 8 and mesh.shape["rep"] == 4
    shards = gathered_plan if compact else split_plan
    in_specs = (
        P("rep", "dom"),
        P("dom", None, None),
        P("dom"),
        P("dom"),
        P("dom"),
        P("dom"),
        P(),
        P(),
        P(),
        P(None, ("dom", "rep")),
    )
    out_specs = (P(None, ("dom", "rep")), P(), P("dom", None), P())
    return jax.shard_map(shards, mesh=mesh, in_specs=in_specs, out_specs=out_specs, check_vma=False)
```

```python
import functools

import jax
import jax.numpy as jnp
from jax import lax
from jax.experimental import pallas as pl
from jax.experimental.pallas import tpu as pltpu
from jax.sharding import PartitionSpec as P

series_zero = 0.3085083
series_one = -0.4305395
series_two = 0.1864784
LEADING = (((0,), (0,)), ((), ()))
TRAILING = (((1,), (1,)), ((), ()))
AXES = ("dom", "rep")
F32 = jnp.float32
BF16 = jnp.bfloat16
VMEM = pl.BlockSpec(memory_space=pltpu.VMEM)
SMEM = pl.BlockSpec(memory_space=pltpu.SMEM)


def pieces(value):
    high = value.astype(BF16)
    rest = value - high.astype(F32)
    middle = rest.astype(BF16)
    low = (rest - middle.astype(F32)).astype(BF16)
    return jnp.concatenate([high, middle, low], axis=0)


def whole(parts):
    rows = parts.shape[0] // 3
    return parts[:rows] + parts[rows : 2 * rows] + parts[2 * rows :]


def open_kernel(place, out):
    out[...] = jnp.full(out.shape, place[0], F32)


def prepare_kernel(segment, block, place, slots, cot, opened, packed, rank_row):
    nodes = slots.shape[1]
    half = nodes // 2
    row = slots[...].astype(F32)
    column = jnp.broadcast_to(row, (8, nodes)).T[:, 0:1]
    wide = jnp.broadcast_to(row, (nodes, nodes))
    order = jnp.sum(jnp.where(column < wide, 1.0, 0.0), axis=0, keepdims=True).astype(jnp.int32)
    target = slots[...] // block
    rank = (target % 2) * half + (target // 2) * segment + order - target * segment
    rank_row[...] = rank
    rank_column = jnp.broadcast_to(rank.astype(F32), (8, nodes)).T[:, 0:1]
    lane = lax.broadcasted_iota(jnp.int32, (nodes, nodes), 1).astype(F32)
    ordered = jnp.sum(jnp.where(rank_column == lane, column, 0.0), axis=0, keepdims=True)
    mine = jnp.where(place[1] % 2 == 0, ordered[:, :half], ordered[:, half:])
    classes, width = cot.shape
    packed[0:classes, :] = cot[...].astype(F32)
    extra = packed.shape[0] - classes
    rows = half // width
    for index in range(rows):
        packed[classes + index : classes + index + 1, :] = mine[:, index * width : (index + 1) * width]
    if extra > rows:
        packed[classes + rows :, :] = jnp.zeros((extra - rows, width), F32)


def operate(place, live, row, col, own, near, far, tiles, field, sums, owners):
    capacity, size, _ = tiles.shape
    count = own.shape[1] // size
    dom = place[0]
    odd = dom % 2
    near_base = (1 - odd) * 2 * count
    far_base = odd * 2 * count
    for index in range(count):
        cut = slice(index * size, (index + 1) * size)
        field[count + index] = pieces(own[:, cut])
        field[near_base + index] = pieces(near[:, cut])
        field[far_base + index] = pieces(far[:, cut])
    total = count * owners
    sums[...] = jnp.zeros_like(sums)
    for slot in range(capacity):
        relative = lax.rem(col[slot] - dom * count + count + total, total)
        product = whole(
            lax.dot_general(field[relative], tiles[slot], TRAILING, preferred_element_type=F32)
        )
        sums[row[slot]] += jnp.where(slot < live[0], product, 0.0)
    return jnp.concatenate([sums[index] for index in range(count)], axis=1)


def first_kernel(owners, place, live, row, col, own, near, far, tiles, first, field, sums):
    first[...] = operate(place, live, row, col, own, near, far, tiles, field, sums, owners)


def second_kernel(
    owners, place, live, row, col, own, near, far, tiles, features, rank_row, mine, other, field, sums
):
    applied = operate(place, live, row, col, own, near, far, tiles, field, sums, owners)
    base = features[...]
    second = 2.0 * applied - base
    diffused = series_zero * base + series_one * own[...] + series_two * second
    nodes = base.shape[1]
    spot = lax.broadcasted_iota(jnp.int32, (nodes, nodes), 0)
    chosen = jnp.where(spot == rank_row[...], 1.0, 0.0).astype(BF16)
    ordered = whole(lax.dot_general(pieces(diffused), chosen, TRAILING, preferred_element_type=F32))
    low, high = ordered[:, : nodes // 2], ordered[:, nodes // 2 :]
    core = place[1] % 2
    mine[...] = jnp.where(core == 0, low, high)
    other[...] = jnp.where(core == 0, high, low)


def cotangent_kernel(orders, classes, segment, place, *refs):
    sources = refs[: len(orders)]
    arranged, slot_rows, held, listed = refs[len(orders) :]
    me = place[0] * 2 + place[1] // 2
    core = place[1] % 2
    blocks = held.shape[0]
    width = held.shape[2]
    parts = arranged.shape[0]
    rows = listed.shape[1]
    for source, order in zip(sources, orders):
        for index, mask in enumerate(order):
            block = jnp.bitwise_xor(me, mask)
            held[block] = source[index, 0:classes, :].astype(BF16)
            listed[block] = source[index, classes : classes + rows, :]
    lists = []
    for part in range(parts):
        listing = listed[2 * part]
        row = jnp.concatenate([listing[i : i + 1] for i in range(rows)], axis=1)
        slot_rows[part] = row
        lists.append(row)
    columns = jnp.concatenate(lists, axis=0).T
    lane = lax.broadcasted_iota(jnp.int32, (segment, width), 1).astype(F32)
    for block in range(blocks):
        start = ((2 * block + core) * width).astype(F32)
        cut = slice(block * segment, (block + 1) * segment)
        chosen = jnp.concatenate(
            [
                jnp.where(columns[cut, part : part + 1] - start == lane, 1.0, 0.0)
                for part in range(parts)
            ],
            axis=0,
        ).astype(BF16)
        moved = lax.dot_general(chosen, held[block], TRAILING, preferred_element_type=F32)
        for part in range(parts):
            arranged[part, cut, :] = moved[part * segment : (part + 1) * segment].astype(BF16)


def activated(pre):
    half = 0.5 * pre
    lift = jnp.tanh(half) + 1.0
    value = half * lift
    return value.astype(BF16), lift + value * (2.0 - lift)


def feature_rows(source, rep):
    replicas = source.shape[0]
    return jnp.concatenate([source[jnp.bitwise_xor(rep, i)] for i in range(replicas)], axis=0)


def forward(inputs, dom, mid_rows, w_in, w_mid):
    pre_one = lax.dot_general(inputs, w_in[...], LEADING, preferred_element_type=F32)
    hidden_one, slope_one = activated(pre_one)
    own_pre = lax.dot_general(
        inputs,
        w_in[:, pl.ds(pl.multiple_of(dom * mid_rows, mid_rows), mid_rows)],
        LEADING,
        preferred_element_type=F32,
    )
    own_hidden, _ = activated(own_pre)
    pre_two = jnp.dot(hidden_one, w_mid[...], preferred_element_type=F32)
    hidden_two, slope_two = activated(pre_two)
    return own_hidden, hidden_two, slope_one, slope_two


def forward_kernel(mid_rows, place, *refs):
    *sources, w_in, w_mid, own_hidden, hidden_two, slope_one, slope_two = refs
    dom, rep = place[0], place[1]
    values = [feature_rows(source, rep).astype(BF16) for source in sources]
    results = forward(jnp.concatenate(values, axis=1), dom, mid_rows, w_in, w_mid)
    for out, result in zip((own_hidden, hidden_two, slope_one, slope_two), results):
        out[...] = result


def train_kernel(fresh, masks, begun, again, finish, place, *refs):
    if again:
        grads_before, batch_before = refs[:2]
        refs = refs[2:]
    sources = refs[: len(masks)]
    refs = refs[len(masks) :]
    states = refs[:4] if begun else ()
    arranged, slot_rows, w_in, w_mid, w_out, grads, batch, *rest = refs[len(states) :]
    mid_rows = grads.shape[0] - arranged.shape[2]
    dom, rep = place[0], place[1]
    width = batch.shape[1]
    replicas = sources[0].shape[0]
    own_start = (dom * replicas + rep) * width
    values, cots = [], []
    moved = batch_before[...] if again else jnp.zeros(batch.shape, F32)
    for source, mask in zip(sources, masks):
        part = jnp.bitwise_xor(dom, mask)
        value = feature_rows(source, rep)
        spot = lax.broadcasted_iota(jnp.int32, (width, value.shape[1]), 0) + own_start
        chosen = jnp.where(spot.astype(F32) == slot_rows[part], 1.0, 0.0).astype(BF16)
        moved = moved + whole(
            lax.dot_general(pieces(value), chosen, TRAILING, preferred_element_type=F32)
        )
        values.append(value.astype(BF16))
        cots.append(arranged[part])
    batch[...] = moved
    inputs = jnp.concatenate(values, axis=1)
    cot = jnp.concatenate(cots, axis=0)
    done = inputs.shape[1] - fresh
    results = forward(inputs[:, done:], dom, mid_rows, w_in, w_mid)
    if begun:
        results = [
            jnp.concatenate([state[...], result], axis=0) for state, result in zip(states, results)
        ]
    own_hidden, hidden_two, slope_one, slope_two = results
    term = lax.dot_general(cot, hidden_two, LEADING, preferred_element_type=F32)
    grads[mid_rows:, :] = grads_before[mid_rows:, :] + term if again else term
    back_two = jnp.dot(cot, w_out[...], preferred_element_type=F32)
    delta_two = (back_two * slope_two).astype(BF16)
    term = lax.dot_general(own_hidden, delta_two, LEADING, preferred_element_type=F32)
    grads[:mid_rows, :] = grads_before[:mid_rows, :] + term if again else term
    if finish:
        rest[0][...] = input_gradient(inputs, delta_two, slope_one, w_mid)
    else:
        for out, value in zip(rest, (inputs, delta_two, slope_one)):
            out[...] = value


def input_gradient(inputs, delta_two, slope_one, w_mid):
    back_one = lax.dot_general(delta_two, w_mid[...], TRAILING, preferred_element_type=F32)
    delta_one = (back_one * slope_one).astype(BF16)
    return jnp.dot(inputs, delta_one, preferred_element_type=F32)


def last_kernel(before, inputs, delta_two, slope_one, w_mid, grad_in):
    grad_in[...] = before[...] + input_gradient(
        inputs[...], delta_two[...], slope_one[...], w_mid
    )


def add_kernel(scales, mine, theirs, *outs):
    start = 0
    for out, scale in zip(outs, scales):
        cut = slice(start, start + out.shape[0])
        out[...] = (mine[cut, :] + theirs[cut, :]) * scale
        start += out.shape[0]


def call(kernel, outs, scalars, arrays, scratch=(), micros=1.5, mib=16):
    cost = pl.CostEstimate(
        flops=int(micros * 1e9), bytes_accessed=int(micros * 3.6e6), transcendentals=0
    )
    return pl.pallas_call(
        kernel,
        out_shape=outs,
        in_specs=[SMEM] * len(scalars) + [VMEM] * len(arrays),
        out_specs=jax.tree.map(lambda _: VMEM, outs),
        scratch_shapes=list(scratch),
        compiler_params=pltpu.CompilerParams(vmem_limit_bytes=mib * 2**20),
        cost_estimate=cost,
    )(*scalars, *arrays)


def exchanged(value, mask, devices):
    return lax.ppermute(value, AXES, [(i, i ^ mask) for i in range(devices)])


def gathered_plan(
    features, tiles, tile_row, tile_col, tile_count, dest_slot, w_in, w_mid, w_out, cotangent
):
    owners, replicas = lax.axis_size("dom"), lax.axis_size("rep")
    devices = owners * replicas
    place = jnp.stack([lax.axis_index("dom"), lax.axis_index("rep")]).astype(jnp.int32)
    scalars = [place, tile_count, tile_row, tile_col]
    feature_count, node_count = features.shape
    size = tiles.shape[1]
    classes, width = cotangent.shape
    hidden = w_in.shape[1]
    segment = node_count // devices
    half = node_count // 2
    count = node_count // size
    send = functools.partial(exchanged, devices=devices)
    far_pairs = [
        (d * replicas + r, ((d + 1 if d % 2 else d - 1) % owners) * replicas + r)
        for d in range(owners)
        for r in range(replicas)
    ]

    def far(value):
        return lax.ppermute(value, AXES, far_pairs)

    rows = half // width
    padded = classes + rows + (-(classes + rows)) % 8
    opened = call(open_kernel, jax.ShapeDtypeStruct((8, 128), F32), [place], [], micros=4.0)
    near_one, far_one = send(features, replicas), far(features)
    packed, rank_row = call(
        functools.partial(prepare_kernel, segment, width),
        (
            jax.ShapeDtypeStruct((padded, width), F32),
            jax.ShapeDtypeStruct((1, node_count), jnp.int32),
        ),
        [place],
        [dest_slot.reshape(1, -1), cotangent, opened],
    )
    field = pltpu.VMEM((3 * count, 3 * feature_count, size), BF16)
    sums = pltpu.VMEM((count, feature_count, size), F32)
    first = call(
        functools.partial(first_kernel, owners),
        jax.ShapeDtypeStruct(features.shape, F32),
        scalars,
        [features, near_one, far_one, tiles],
        [field, sums],
    )
    line = [packed] + [send(packed, m) for m in (8, 16, 24)]
    column = jnp.stack(line)
    near_two, far_two = send(first, replicas), far(first)
    across_y, across_x = send(jnp.stack(line[0:3]), 2), send(column, 4)
    corner_one = send(across_y, 4)
    corner_two = send(jnp.concatenate([column[3:4], across_x[3:4]]), 2)
    mine, other = call(
        functools.partial(second_kernel, owners),
        tuple(jax.ShapeDtypeStruct((feature_count, half), F32) for _ in range(2)),
        scalars,
        [first, near_two, far_two, tiles, features, rank_row],
        [field, sums],
    )
    own = jnp.stack([mine, send(other, 1), send(mine, 2), send(other, 3)])
    facing = send(own, 4)
    ring = [send(own, m) for m in (24, 16)]
    near_line = send(own, 8)
    mid_rows = hidden // owners
    begun = call(
        functools.partial(forward_kernel, mid_rows),
        (
            jax.ShapeDtypeStruct((3 * half, mid_rows), BF16),
            jax.ShapeDtypeStruct((3 * half, hidden), BF16),
            jax.ShapeDtypeStruct((3 * half, hidden), F32),
            jax.ShapeDtypeStruct((3 * half, hidden), F32),
        ),
        [place],
        [own, facing, near_line, w_in, w_mid],
        micros=3.7,
        mib=20,
    )
    orders = ((0, 4, 8, 12), (1, 5, 9), (2, 6, 10, 14), (3, 7, 11), (13, 15))
    arranged, slot_rows = call(
        functools.partial(cotangent_kernel, orders, classes, segment),
        (
            jax.ShapeDtypeStruct((owners, half, classes), BF16),
            jax.ShapeDtypeStruct((owners, 1, half), F32),
        ),
        [place],
        [column, across_y, across_x, corner_one, corner_two],
        [
            pltpu.VMEM((devices // 2, classes, width), BF16),
            pltpu.VMEM((devices // 2, rows, width), F32),
        ],
    )
    near_ready, *begun = lax.optimization_barrier((near_line, *begun))
    near_across = send(near_ready, 4)
    *ring, gate, slot_rows = lax.optimization_barrier((*ring, begun[0], slot_rows))
    begun = (gate, *begun[1:])
    last = send(jnp.stack(ring), 4)

    feats = feature_count * replicas
    mid_shape = jax.ShapeDtypeStruct((mid_rows, hidden), F32)
    out_shape = jax.ShapeDtypeStruct((classes, hidden), F32)
    grads_shape = jax.ShapeDtypeStruct((mid_rows + classes, hidden), F32)
    in_shape = jax.ShapeDtypeStruct((feats, hidden), F32)
    batch_shape = jax.ShapeDtypeStruct((feats, width), F32)

    def train(before, sources, masks, states, finish, mib):
        fresh = half * (len(masks) - 3 * bool(states))
        rows = half * len(masks)
        rest = (
            (in_shape,)
            if finish
            else (
                jax.ShapeDtypeStruct((feats, rows), BF16),
                jax.ShapeDtypeStruct((rows, hidden), BF16),
                jax.ShapeDtypeStruct((rows, hidden), F32),
            )
        )
        return call(
            functools.partial(train_kernel, fresh, masks, bool(states), bool(before), finish),
            (grads_shape, batch_shape, *rest),
            [place],
            [*before, *sources, *states, arranged, slot_rows, w_in, w_mid, w_out],
            micros=2.5 * len(masks),
            mib=mib,
        )

    grads_before, batch_before, in_before = train(
        (), [own, facing, near_line, *ring], (0, 1, 2, 6, 4), begun, True, 32
    )
    grads, batch_features, *rest = train(
        (grads_before, batch_before), [near_across, last[0], last[1]], (3, 7, 5), (), False, 20
    )
    theirs = send(grads, 1)
    grad_in = call(last_kernel, in_shape, [], [in_before, *rest, w_mid], micros=2.5, mib=12)
    their_in = send(grad_in, 1)
    grad_mid, grad_out = call(
        functools.partial(add_kernel, (0.5, 1.0)), (mid_shape, out_shape), [], [grads, theirs]
    )
    their_in, grad_mid = lax.optimization_barrier((their_in, grad_mid))
    grad_in = call(functools.partial(add_kernel, (0.25,)), (in_shape,), [], [grad_in, their_in])[0]
    return batch_features, grad_in, grad_mid, grad_out


def extended_2(cells, sides, width):
    for axis, dim in sides:
        count = lax.axis_size(axis)
        head = lax.slice_in_dim(cells, 0, width, axis=dim)
        tail = lax.slice_in_dim(cells, cells.shape[dim] - width, cells.shape[dim], axis=dim)
        cells = jnp.concatenate(
            [
                lax.ppermute(tail, axis, [(i, (i + 1) % count) for i in range(count)]),
                cells,
                lax.ppermute(head, axis, [((i + 1) % count, i) for i in range(count)]),
            ],
            axis=dim,
        )
    return cells


def silu_slope(pre):
    sigma = jax.nn.sigmoid(pre)
    return sigma * (1.0 + pre * (1.0 - sigma))


def neighbour_blocks(local, margin, tile_size):
    extended = extended_2(local, (("dom", 1),), margin * tile_size)
    return extended


def apply_operator(local, tiles_across, assignment_map, relative, margin):
    feature_count, node_count = local.shape
    tile_size = tiles_across.shape[1]
    extended = neighbour_blocks(local, margin, tile_size)
    blocks = extended.reshape(feature_count, -1, tile_size)
    input_values = jnp.take(blocks, relative, axis=1)
    block_products = jnp.einsum(
        "lkz,glz->glk", tiles_across, input_values, precision=lax.Precision.HIGHEST
    )
    final_result = jnp.einsum(
        "wy,kya->kwa", assignment_map, block_products, precision=lax.Precision.HIGHEST
    )
    return final_result.reshape(feature_count, node_count)


def split_plan(
    features, tiles, tile_row, tile_col, tile_count, dest_slot, w_in, w_mid, w_out, cotangent
):
    node_partition = lax.axis_index("dom")
    owners = lax.axis_size("dom")
    replicas = lax.axis_size("rep")
    feature_count, node_count = features.shape
    capacity = tiles.shape[0]
    tile_size = tiles.shape[1]
    block_count = node_count // tile_size
    total_blocks = block_count * owners
    relative = jnp.mod(tile_col - node_partition * block_count + block_count, total_blocks)
    live_mask = (jnp.arange(capacity, dtype=jnp.int32) < tile_count[0]).astype(jnp.float32)
    assignment_map = (
        tile_row[None, :] == jnp.arange(block_count, dtype=jnp.int32)[:, None]
    ).astype(jnp.float32) * live_mask[None, :]
    tiles_across = tiles.astype(jnp.float32)
    first = apply_operator(features, tiles_across, assignment_map, relative, block_count)
    second = (
        2.0 * apply_operator(first, tiles_across, assignment_map, relative, block_count) - features
    )
    diffused = series_zero * features + series_one * first + series_two * second
    segment = node_count // (owners * replicas)
    batch_rows = node_count // replicas
    sort_order = jnp.argsort(dest_slot)
    sorted_slots = jnp.take(dest_slot, sort_order)
    moved_rows = jnp.take(diffused, sort_order, axis=1).reshape(
        feature_count, owners, replicas, segment
    )
    moved_slots = sorted_slots.astype(jnp.float32).reshape(1, owners, replicas, segment)
    arrived, arrived_slots = (
        lax.all_to_all(
            lax.all_to_all(moved_rows, "dom", split_axis=1, concat_axis=1, tiled=True),
            "rep",
            split_axis=2,
            concat_axis=0,
            tiled=True,
        ),
        lax.all_to_all(
            lax.all_to_all(moved_slots, "dom", split_axis=1, concat_axis=1, tiled=True),
            "rep",
            split_axis=2,
            concat_axis=0,
            tiled=True,
        ),
    )
    owner_index = node_partition * replicas + lax.axis_index("rep")
    local_slots = arrived_slots[0].reshape(-1).astype(jnp.int32) - owner_index * batch_rows
    gathered = arrived.reshape(feature_count * replicas, -1)
    batch_features = jnp.zeros(gathered.shape, jnp.float32).at[:, local_slots].set(gathered)
    inputs_bf = batch_features.astype(jnp.bfloat16)
    pre_one = lax.dot_general(inputs_bf, w_in, LEADING, preferred_element_type=jnp.float32)
    hidden_one = jax.nn.silu(pre_one).astype(jnp.bfloat16)
    pre_two = jnp.dot(hidden_one, w_mid, preferred_element_type=jnp.float32)
    hidden_two = jax.nn.silu(pre_two).astype(jnp.bfloat16)
    grad_out = jnp.dot(cotangent, hidden_two, preferred_element_type=jnp.float32)
    back_two = lax.dot_general(cotangent, w_out, LEADING, preferred_element_type=jnp.float32)
    delta_two = (back_two * silu_slope(pre_two)).astype(jnp.bfloat16)
    back_one = lax.dot_general(delta_two, w_mid, TRAILING, preferred_element_type=jnp.float32)
    delta_one = (back_one * silu_slope(pre_one)).astype(jnp.bfloat16)
    grad_in = jnp.dot(inputs_bf, delta_one, preferred_element_type=jnp.float32)
    mid_shard = lax.psum_scatter(
        lax.dot_general(hidden_one, delta_two, LEADING, preferred_element_type=jnp.float32),
        "dom",
        scatter_dimension=0,
        tiled=True,
    )
    grad_mid = lax.psum(mid_shard, "rep")
    grad_in, grad_out = lax.psum((grad_in, grad_out), ("dom", "rep"))
    return (batch_features, grad_in, grad_mid, grad_out)


def solution(mesh):
    compact = mesh.shape["dom"] == 8 and mesh.shape["rep"] == 4
    shards = gathered_plan if compact else split_plan
    in_specs = (
        P("rep", "dom"),
        P("dom", None, None),
        P("dom"),
        P("dom"),
        P("dom"),
        P("dom"),
        P(),
        P(),
        P(),
        P(None, ("dom", "rep")),
    )
    out_specs = (P(None, ("dom", "rep")), P(), P("dom", None), P())
    return jax.shard_map(shards, mesh=mesh, in_specs=in_specs, out_specs=out_specs, check_vma=False)
```
